256 devices in a mesh: row: 64 (over z, x_lo, y), col: 4 (over x_hi, core).
Axes of the slice: x: 4 (x_hi: 2, x_lo: 2; x = x_hi * 2 + x_lo), y: 4, z: 8, core: 2. Of those that a mesh axis runs over, the one named last changes fastest.
Arguments:
- pair: bfloat16 [768, 768, 128], P('row', 'col'), may hold values from -6 to 6
- residue_mask: int32 [768], replicated, may hold values 0 or 1
- in_gain: float32 [2, 128], replicated, may hold values from 0.5 to 2
- w_in: bfloat16 [2, 5, 128, 128], replicated, may hold values from -0.5 to 0.5
- out_gain: float32 [2, 128], replicated, may hold values from 0.5 to 2
- w_out: bfloat16 [2, 128, 128], replicated, may hold values from -0.5 to 0.5
Outputs:
- pair_out: bfloat16 [768, 768, 128], P('row', 'col')
The draws below stay inside these ranges and needn't reach their ends.
All inputs are finite; a program needn't handle non-finite values.
Results may differ from the reference program's by a relative error of at most 0.02.
Values may be sent and summed in bfloat16 or wider, within the bound.
A program may use at most 64 MiB of HBM per device.

```python
import math
import jax
import jax.numpy as jnp
from jax import lax

C = 128
NRES = 768


def plant(values, stream_key, least, largest):
    longest = values.shape.index(max(values.shape))
    spots = []
    for shift in (0, 1):
        where = [jax.random.randint(jax.random.fold_in(stream_key, axis), (), 0, length) for axis, length in enumerate(values.shape)]
        where[longest] = (where[longest] + shift) % values.shape[longest]
        spots.append(tuple(where))
    return values.at[spots[0]].set(least).at[spots[1]].set(largest)


def shard_levels(stream_key, dims, pieces, least, high):
    def one(position, shards_of):
        steps = jax.random.uniform(jax.random.fold_in(jax.random.fold_in(stream_key, 6), position), (shards_of,), jnp.float32, least / len(pieces), high / len(pieces))
        return jnp.repeat(jnp.exp(steps), dims[position] // shards_of).reshape((-1,) + (1,) * (len(dims) - position - 1))

    level = one(*pieces[0])
    for cut in pieces[1:]:
        level = level * one(*cut)
    return level


def bell_draw(rng, dims, deviation, bound, cuts=(), held_as=jnp.bfloat16):
    factor_of = shard_levels(rng, dims, cuts, -0.22, 0.18) if cuts else 1.0
    entries = jax.random.normal(rng, dims, jnp.float32) * deviation * factor_of
    return jnp.minimum(jnp.maximum(entries, -bound), bound).astype(held_as)


def setup_inputs(seed: int = 0) -> dict:
    splits = jax.random.split(jax.random.key(seed), 7)
    return {
        "pair": bell_draw(splits[0], (NRES, NRES, C), 1.0, 6.0, ((0, 64), (1, 4))),
        "residue_mask": plant((jax.random.randint(splits[1], (NRES,), 0, 8) < 7).astype(jnp.int32), jax.random.fold_in(splits[1], 1), 0, 1),
        "in_gain": jnp.clip(jnp.exp(jax.random.uniform(splits[2], (2, C), jnp.float32, math.log(0.5), math.log(2.0))), 0.5, 2.0),
        "w_in": bell_draw(splits[3], (2, 5, C, C), C ** -0.5, 0.5),
        "out_gain": jnp.clip(jnp.exp(jax.random.uniform(splits[4], (2, C), jnp.float32, math.log(0.5), math.log(2.0))), 0.5, 2.0),
        "w_out": bell_draw(splits[5], (2, C, C), C ** -0.5, 0.5),
    }


def layer_norm(values, gain):
    center = lax.optimization_barrier(jnp.mean(values, axis=-1, keepdims=True))
    shifted = values - center
    spread = lax.optimization_barrier(jnp.mean(shifted * shifted, axis=-1, keepdims=True))
    return shifted * lax.rsqrt(spread + 1e-05) * gain

def one_update(state, mask_vals, gain_in, weights_in, gain_out, weight_out, outgoing):
    span = NRES // 8
    channels = C

    def project(inputs):
        block, block_mask = inputs
        normed = layer_norm(block.astype(jnp.float32), gain_in).astype(jnp.bfloat16)
        projected = jnp.einsum('rnc,vcd->vdrn', normed.astype(jnp.float32), weights_in.astype(jnp.float32))
        pair_mask = block_mask[:, None] * mask_vals[None, :]
        left_side = (jax.nn.sigmoid(projected[0]) * projected[1] * pair_mask).astype(jnp.bfloat16)
        right_side = (jax.nn.sigmoid(projected[2]) * projected[3] * pair_mask).astype(jnp.bfloat16)
        gate_vals = jax.nn.sigmoid(projected[4])
        return (left_side, right_side, gate_vals)
    left_side, right_side, gate_vals = lax.map(project, (state.reshape(8, span, NRES, channels), mask_vals.reshape(8, span)))
    left_side = left_side.transpose(1, 0, 2, 3).reshape(channels, NRES, NRES)
    right_side = right_side.transpose(1, 0, 2, 3).reshape(channels, NRES, NRES)
    group = 8

    def triangle(inputs):
        left_part, right_part = inputs
        if outgoing:
            summed = jnp.einsum('cik,cjk->cij', left_part.astype(jnp.float32), right_part.astype(jnp.float32))
        else:
            summed = jnp.einsum('cki,ckj->cij', left_part.astype(jnp.float32), right_part.astype(jnp.float32))
        return summed.astype(jnp.bfloat16)
    product = lax.map(triangle, (left_side.reshape(channels // group, group, NRES, NRES), right_side.reshape(channels // group, group, NRES, NRES)))
    product = product.reshape(channels, 8, span, NRES).transpose(1, 0, 2, 3)

    def finish(inputs):
        tri_block, gate_block, state_block = inputs
        tri_normed = layer_norm(tri_block.astype(jnp.float32).transpose(1, 2, 0), gain_out).astype(jnp.bfloat16)
        update_term = jnp.einsum('rnc,cd->rnd', tri_normed.astype(jnp.float32), weight_out.astype(jnp.float32))
        update_term = update_term * gate_block.transpose(1, 2, 0)
        return (state_block.astype(jnp.float32) + update_term).astype(jnp.bfloat16)
    result = lax.map(finish, (product, gate_vals, state.reshape(8, span, NRES, channels)))
    return result.reshape(NRES, NRES, channels)

def reference(pair, residue_mask, in_gain, w_in, out_gain, w_out):
    mask_vals = residue_mask.astype(jnp.float32)
    first = one_update(pair, mask_vals, in_gain[0], w_in[0], out_gain[0], w_out[0], True)
    return one_update(first, mask_vals, in_gain[1], w_in[1], out_gain[1], w_out[1], False)
```

```python
import functools

import jax
import jax.numpy as jnp
from jax import lax
from jax.experimental import pallas as pl
from jax.experimental.pallas import tpu as pltpu
from jax.sharding import PartitionSpec as P

MESH = pl.DeviceIdType.MESH
F32 = jnp.float32
BF16 = jnp.bfloat16
ROWS = 64
CH = 128
IL = 6
CHUNKS = 4
CW = CH // CHUNKS
NT = (((1,), (1,)), ((), ()))
NN = (((1,), (0,)), ((), ()))
TN = (((0,), (0,)), ((), ()))


def dot(a, b, dims):
    return lax.dot_general(a, b, dims, preferred_element_type=F32)


def kernel(
    pair_ref, mask_s, mask_v, in_gain, w_in, out_gain, w_out, out_ref,
    zin, zbuf, xn, gate, wt, bf, b, lr0, lr1, rc, lt, sel, selt, xs, xp, ts, tri, tf, gcol, pm,
    x_send, x_recv, lr_send, lr_recv, t_send, t_recv,
):
    r = lax.axis_index("row")
    q = lax.axis_index("col")
    xhi = q // 2
    c = q % 2
    partner = (r, xhi * 2 + 1 - c)
    z_me = r // 8
    chip = r * 2 + xhi

    lr0[...] = jnp.zeros_like(lr0)
    lr1[...] = jnp.zeros_like(lr1)

    barrier = pltpu.get_barrier_semaphore()

    @pl.loop(1, 256)
    def _(s):
        t = (r * 4 + q + s) % 256
        pl.semaphore_signal(barrier, inc=1, device_id=(t // 4, t % 4), device_id_type=MESH)

    for u in range(2):
        for v in range(4):
            turned = w_in[u, v].astype(F32).T.astype(BF16)
            for g in range(CHUNKS):
                wt[u, g, v * CW : (v + 1) * CW, :] = turned[g * CW : (g + 1) * CW]
        gcol[u] = jnp.broadcast_to(out_gain[u : u + 1, :], (CH, CH)).T
    row_id = lax.broadcasted_iota(jnp.int32, (512, 384), 0)
    col_id = lax.broadcasted_iota(jnp.int32, (512, 384), 1)
    hit = (row_id % 8 < IL) & ((row_id // 8) * IL + row_id % 8 == col_id)
    sel[...] = jnp.where(hit, 1.0, 0.0).astype(BF16)
    row_id = lax.broadcasted_iota(jnp.int32, (384, 512), 1)
    col_id = lax.broadcasted_iota(jnp.int32, (384, 512), 0)
    hit = (row_id % 8 < IL) & ((row_id // 8) * IL + row_id % 8 == col_id)
    selt[...] = jnp.where(hit, 1.0, 0.0).astype(BF16)
    for k in range(3):
        cols = mask_v[pl.ds(xhi * 3 + k, 1), :].astype(F32)
        for i in range(IL):
            pm[i : i + 1, k * 128 : (k + 1) * 128] = cols * mask_s[r * 12 + c * IL + i].astype(F32)

    pl.semaphore_wait(barrier, 255)

    swap = pltpu.make_async_remote_copy(
        pair_ref.at[pl.ds((1 - c) * IL, IL)], zin.at[...], x_send.at[0], x_recv.at[0],
        device_id=partner, device_id_type=MESH,
    )
    swap.start()
    zbuf[:, pl.ds(pl.multiple_of(c * 192, 64), 192), :] = pair_ref[pl.ds(c * IL, IL)]
    swap.wait()
    zbuf[:, pl.ds(pl.multiple_of((1 - c) * 192, 64), 192), :] = zin[...]

    for u in range(2):
        lr = (lr0, lr1)[u]

        @pl.loop(0, IL)
        def _(i):
            val = zbuf[i].astype(F32)
            shifted = val - jnp.mean(val, axis=-1, keepdims=True)
            spread = jnp.mean(shifted * shifted, axis=-1, keepdims=True)
            xn[i] = (shifted * lax.rsqrt(spread + 1e-05) * in_gain[u : u + 1, :]).astype(BF16)

        if u == 0:
            core_to, slot = xhi, lambda: lr0.at[:, :, r * 2 + c, pl.ds(0, IL), :]
            is_self = xhi == c
        else:
            core_to, slot = c, lambda: lr1.at[:, pl.ds(xhi * 3, 3), r, pl.ds(0, IL), :]
            is_self = c == c

        @pl.loop(0, CHUNKS)
        def _(step):
            g = (z_me // 2 + 2 + step) % CHUNKS

            @pl.loop(0, IL)
            def _(i):
                o = dot(wt[u, g], xn[i], NT)
                mask = pm[pl.ds(i, 1), :]
                for s in range(2):
                    side = jax.nn.sigmoid(o[2 * s * CW : (2 * s + 1) * CW])
                    side = side * o[(2 * s + 1) * CW : (2 * s + 2) * CW] * mask
                    for k in range(3):
                        bf[s, k, pl.ds(i, CW, stride=8), :] = side[:, k * 128 : (k + 1) * 128]

            for s in range(2):
                for k in range(3):
                    b[pl.ds(g * CW, CW), s, k] = bf[s, k].reshape(CW, 8, 128).astype(BF16)

            @pl.loop(0, CW)
            def _(n):
                m = g * CW + (n + chip) % CW
                src = b.at[m, :, :, pl.ds(0, IL), :]
                mine = (m == chip) & is_self

                @pl.when(mine)
                def _():
                    pltpu.make_async_copy(src, slot(), lr_recv.at[u]).start()

                @pl.when(jnp.logical_not(mine))
                def _():
                    pltpu.make_async_remote_copy(
                        src, slot(), lr_send.at[u], lr_recv.at[u],
                        device_id=(m // 2, (m % 2) * 2 + core_to), device_id_type=MESH,
                    ).start()

        @pl.loop(0, IL)
        def _(i):
            gate[i] = jax.nn.sigmoid(dot(xn[i], w_in[u, 4], NN))

        whole = b.at[:, :, :, pl.ds(0, IL), :]
        most = b.at[pl.ds(0, CH - 1), :, :, pl.ds(0, IL), :]
        one = b.at[0, :, :, pl.ds(0, IL), :]
        pltpu.make_async_copy(whole, whole, lr_recv.at[u]).wait()
        pltpu.make_async_copy(most, most, lr_send.at[u]).wait()
        if u == 0:
            @pl.when(jnp.logical_not(is_self))
            def _():
                pltpu.make_async_copy(one, one, lr_send.at[u]).wait()

        if u == 0:
            for half in range(2):
                part = [lr0[1, k, 64 * half : 64 * half + 64].reshape(512, 128) for k in range(3)]
                rc[384 * half : 384 * half + 384, :] = dot(
                    selt[...], jnp.concatenate(part, axis=1), NN
                ).astype(BF16)

            def product(h, n):
                at = pl.ds(h * 64 + n * 16, 16)
                left = [lr0[0, k, at].reshape(128, 128) for k in range(3)]
                return dot(jnp.concatenate(left, axis=1), rc[...], NT)
        else:
            for half in range(2):
                part = [lr1[0, half * 3 + k].reshape(512, 128) for k in range(3)]
                lt[half] = dot(sel[...], jnp.concatenate(part, axis=1), NT).astype(BF16)

            def product(h, n):
                left = lt[h, pl.ds(pl.multiple_of(n * 128, 128), 128)]
                right = [lr1[1, k].reshape(512, 128) for k in range(6)]
                return dot(left, jnp.concatenate(right, axis=1), NN)

        @pl.loop(0, 4)
        def _(n):
            xs[u, pl.ds(pl.multiple_of(n * 128, 128), 128), :] = product(1 - c, n).astype(BF16)

        give = pltpu.make_async_remote_copy(
            xs.at[u], xp.at[u], x_send.at[1 + u], x_recv.at[1 + u],
            device_id=partner, device_id_type=MESH,
        )
        give.start()
        give.wait()

        here = r // 32 == c

        @pl.loop(0, 4)
        def _(step):
            n = (z_me + 2 + step) % 4
            p = product(c, n) + xp[u, pl.ds(pl.multiple_of(n * 128, 128), 128), :].astype(F32)
            for h in range(2):
                for k in range(3):
                    tile = p[:, (h * 3 + k) * 128 : (h * 3 + k + 1) * 128]
                    ts[u, pl.ds(n * 16, 16), h, k] = tile.reshape(16, 8, 128).astype(BF16)

            @pl.loop(0, 32)
            def _(s):
                t = (s + chip * 2 + c) % 32
                e = n * 16 + t // 2
                h = t % 2
                to_r = c * 32 + e // 2
                to_q = h * 2 + e % 2
                src = ts.at[u, e, h, :, pl.ds(0, IL), :]
                dst = tri.at[u, :, chip, pl.ds(0, IL), :]
                mine = (to_r == r) & (to_q == q)

                @pl.when(mine)
                def _():
                    pltpu.make_async_copy(src, dst, t_recv.at[u]).start()

                @pl.when(jnp.logical_not(mine))
                def _():
                    pltpu.make_async_remote_copy(
                        src, dst, t_send.at[u], t_recv.at[u],
                        device_id=(to_r, to_q), device_id_type=MESH,
                    ).start()

        whole = tri.at[u, :, :, pl.ds(0, IL), :]
        most = tri.at[u, :, pl.ds(0, CH - 1), pl.ds(0, IL), :]
        one = tri.at[u, :, 0, pl.ds(0, IL), :]
        pltpu.make_async_copy(whole, whole, t_recv.at[u]).wait()

        @pl.loop(0, 3)
        def _(k):
            tf[...] = tri[u, k].astype(F32).reshape(CH * 8, 128)
            at = pl.ds(pl.multiple_of(k * 128, 128), 128)
            for i in range(IL):
                val = tf[pl.ds(i, CH, stride=8), :]
                shifted = val - jnp.mean(val, axis=0, keepdims=True)
                spread = jnp.mean(shifted * shifted, axis=0, keepdims=True)
                normed = (shifted * lax.rsqrt(spread + 1e-05) * gcol[u]).astype(BF16)
                term = dot(normed, w_out[u], TN) * gate[i, at, :]
                zbuf[i, at, :] = (zbuf[i, at, :].astype(F32) + term).astype(BF16)

        pltpu.make_async_copy(most, most, t_send.at[u]).wait()

        @pl.when(jnp.logical_not(here))
        def _():
            pltpu.make_async_copy(one, one, t_send.at[u]).wait()

    back = pltpu.make_async_remote_copy(
        zbuf.at[:, pl.ds(pl.multiple_of((1 - c) * 192, 64), 192), :], out_ref.at[pl.ds(c * IL, IL)],
        x_send.at[3], x_recv.at[3], device_id=partner, device_id_type=MESH,
    )
    back.start()
    out_ref[pl.ds(c * IL, IL)] = zbuf[:, pl.ds(pl.multiple_of(c * 192, 64), 192), :]
    back.wait()


def on_device(pair, residue_mask, in_gain, w_in, out_gain, w_out):
    vmem = pl.BlockSpec(memory_space=pltpu.VMEM)
    smem = pl.BlockSpec(memory_space=pltpu.SMEM)
    dma = pltpu.SemaphoreType.DMA
    return pl.pallas_call(
        kernel,
        out_shape=jax.ShapeDtypeStruct(pair.shape, BF16),
        in_specs=[vmem, smem, vmem, vmem, vmem, vmem, vmem],
        out_specs=vmem,
        scratch_shapes=[
            pltpu.VMEM((IL, 192, CH), BF16),
            pltpu.VMEM((IL, 384, CH), BF16),
            pltpu.VMEM((IL, 384, CH), BF16),
            pltpu.VMEM((IL, 384, CH), F32),
            pltpu.VMEM((2, CHUNKS, 4 * CW, CH), BF16),
            pltpu.VMEM((2, 3, CW * 8, 128), F32),
            pltpu.VMEM((CH, 2, 3, 8, 128), BF16),
            pltpu.VMEM((2, 3, 128, 8, 128), BF16),
            pltpu.VMEM((2, 6, 64, 8, 128), BF16),
            pltpu.VMEM((768, 384), BF16),
            pltpu.VMEM((2, 512, 512), BF16),
            pltpu.VMEM((512, 384), BF16),
            pltpu.VMEM((384, 512), BF16),
            pltpu.VMEM((2, 512, 768), BF16),
            pltpu.VMEM((2, 512, 768), BF16),
            pltpu.VMEM((2, 64, 2, 3, 8, 128), BF16),
            pltpu.VMEM((2, 3, CH, 8, 128), BF16),
            pltpu.VMEM((CH * 8, 128), F32),
            pltpu.VMEM((2, CH, 128), F32),
            pltpu.VMEM((8, 384), F32),
            dma((4,)), dma((4,)), dma((2,)), dma((2,)), dma((2,)), dma((2,)),
        ],
        compiler_params=pltpu.CompilerParams(
            collective_id=0, has_side_effects=True, vmem_limit_bytes=48 * 2**20
        ),
        name="triangle",
    )(pair, residue_mask, residue_mask.reshape(6, 128), in_gain, w_in, out_gain, w_out)


def solution(mesh):
    placed = (P("row", "col", None), P(), P(), P(), P(), P())
    return jax.shard_map(
        on_device, mesh=mesh, in_specs=placed, out_specs=P("row", "col", None), check_vma=False
    )
```

```python
import jax
import jax.numpy as jnp
from jax import lax
from jax.experimental import pallas as pl
from jax.experimental.pallas import tpu as pltpu
from jax.sharding import PartitionSpec as P

MESH = pl.DeviceIdType.MESH
F32 = jnp.float32
BF16 = jnp.bfloat16
CH = 128
IL = 6
CHUNKS = 4
CW = CH // CHUNKS
NT = (((1,), (1,)), ((), ()))
NN = (((1,), (0,)), ((), ()))
TN = (((0,), (0,)), ((), ()))


def dot(a, b, dims):
    return lax.dot_general(a, b, dims, preferred_element_type=F32)


def sigmoid(v):
    return 0.5 * jnp.tanh(0.5 * v) + 0.5


def halves(a, b):
    return jnp.concatenate([a, b], axis=1)


def kernel(
    pair_hbm, mask_hbm, mask6_hbm, in_gain_hbm, w_in_hbm, out_gain_hbm, w_out_hbm, out_ref,
    pair, mask_s, mask_v, in_gain, w_in, out_gain, w_out,
    zin, zbuf, zown, xn, gate, wt, bf, b, lr0, lr1, rc, lt, tl, sel, selt, xs0, xp0, xs1, xp1,
    ts, tri, tf, gcol, pm, ones,
    in_sem, x_send, x_recv, p_send, p_recv, lr_send, lr_recv, t_send, t_recv,
):
    r = lax.axis_index("row")
    q = lax.axis_index("col")
    xhi = q // 2
    c = q % 2
    partner = (r, xhi * 2 + 1 - c)
    chip = r * 2 + xhi
    main_at = pl.ds(pl.multiple_of(c * 64, 64), 128)
    tail_at = pl.ds(pl.multiple_of((1 - c) * 128, 128), 64)
    mine_at = pl.ds(pl.multiple_of(c * 192, 64), 192)
    other_at = pl.ds(pl.multiple_of((1 - c) * 192, 64), 192)
    six = pl.ds(0, IL)

    loads = [
        pltpu.make_async_copy(src, dst, in_sem.at[n])
        for n, (src, dst) in enumerate(
            (
                (pair_hbm, pair), (mask_hbm, mask_s), (mask6_hbm, mask_v), (in_gain_hbm, in_gain),
                (w_in_hbm, w_in), (out_gain_hbm, out_gain), (w_out_hbm, w_out),
            )
        )
    ]
    for load in loads:
        load.start()

    lr0[1] = jnp.zeros(lr0.shape[1:], BF16)
    lr1[...] = jnp.zeros_like(lr1)

    bits = [r // 2**k % 2 for k in range(4)]

    def chunk_of(step):
        zh = r // 16
        b1, b0 = 1 - step // 2, 1 - step % 2
        return 2 * ((zh // 2 + b1) % 2) + (zh % 2 + b0) % 2

    def chips(g, last, visit):
        @pl.loop(0, 4)
        def _(hi):
            b3, b2 = 1 - hi // 2, 1 - hi % 2
            base = g * 16 + 8 * ((bits[3] + b3) % 2) + 4 * ((bits[2] + b2) % 2)
            for low in range(7, -1, -1):
                e = base
                for k in range(2):
                    e = e + 2**k * (1 - bits[k] if low >> (k + 1) & 1 else bits[k])
                h = 1 - xhi if low & 1 else xhi
                visit(e, h, low == 0 and last & (hi == 3))

    barrier = pltpu.get_barrier_semaphore()
    pl.semaphore_signal(barrier, inc=1, device_id=partner, device_id_type=MESH)

    @pl.loop(0, CHUNKS)
    def _(step):
        def greet(e, h, mine):
            def signal():
                pl.semaphore_signal(barrier, inc=1, device_id=(e, h * 2 + c), device_id_type=MESH)

            if mine is False:
                signal()
            else:
                pl.when(jnp.logical_not(mine))(signal)

        chips(chunk_of(step), step == 3, greet)

    for load in loads:
        load.wait()

    def turn(u):
        for v in range(4):
            turned = w_in[u, v].astype(F32).T.astype(BF16)
            for g in range(CHUNKS):
                wt[u, g, v * CW : (v + 1) * CW, :] = turned[g * CW : (g + 1) * CW]
        gcol[u] = jnp.broadcast_to(out_gain[u : u + 1, :], (CH, CH)).T

    def norm(u):
        @pl.loop(0, IL)
        def _(i):
            val = zbuf[i]
            shifted = val.astype(F32) - dot(val, ones[...], NN) * (1.0 / CH)
            spread = dot((shifted * shifted).astype(BF16), ones[...], NN) * (1.0 / CH)
            xn[i] = (shifted * lax.rsqrt(spread + 1e-05) * in_gain[u : u + 1, :]).astype(BF16)

    def gates(u):
        @pl.loop(0, IL)
        def _(i):
            gate[i] = sigmoid(dot(xn[i], w_in[u, 4], NN))

    def to_own(src):
        @pl.loop(0, IL)
        def _(i):
            zbuf[i, 0:128] = src[i, main_at]
            zbuf[i, 128:256] = src[IL + i, main_at]
            zbuf[i, 256:320] = src[i, tail_at]
            zbuf[i, 320:384] = src[IL + i, tail_at]

    def project(u, g):
        @pl.loop(0, IL)
        def _(i):
            o = dot(wt[u, g], xn[i], NT)
            mask = pm[u, pl.ds(i, 1), :]
            for s in range(2):
                side = sigmoid(o[2 * s * CW : (2 * s + 1) * CW])
                side = side * o[(2 * s + 1) * CW : (2 * s + 2) * CW] * mask
                for k in range(3):
                    bf[s, k, pl.ds(i, CW, stride=8), :] = side[:, k * 128 : (k + 1) * 128]

        for s in range(2):
            for k in range(3):
                b[pl.ds(g * CW, CW), s, k] = bf[s, k].reshape(CW, 8, 128).astype(BF16)

    def send(src, dst, send_sem, recv_sem, to, mine):
        def remote():
            pltpu.make_async_remote_copy(
                src, dst, send_sem, recv_sem, device_id=to, device_id_type=MESH
            ).start()

        if mine is False:
            remote()
        else:
            pl.when(jnp.logical_not(mine))(remote)

            @pl.when(mine)
            def _():
                pltpu.make_async_copy(src, dst, recv_sem).start()

    lane = lax.broadcasted_iota(jnp.int32, (1, 128), 1)
    row_mask = [mask_s[r * 12 + i].astype(F32) for i in range(2 * IL)]
    main = mask_v[pl.ds(xhi * 3 + 2 * c, 1), :].astype(F32)
    tile = mask_v[pl.ds(xhi * 3 + 1, 1), :].astype(F32)
    swapped = halves(tile[:, 64:], tile[:, :64])
    tail = jnp.where((lane < 64) == (c == 0), tile, swapped)
    for i in range(IL):
        pm[0, i : i + 1, 0:128] = main * row_mask[i]
        pm[0, i : i + 1, 128:256] = main * row_mask[IL + i]
        pm[0, i : i + 1, 256:384] = tail * jnp.where(lane < 64, row_mask[i], row_mask[IL + i])
        for k in range(3):
            cols = mask_v[pl.ds(xhi * 3 + k, 1), :].astype(F32)
            pm[1, i : i + 1, k * 128 : (k + 1) * 128] = cols * jnp.where(
                c == 0, row_mask[i], row_mask[IL + i]
            )

    ones[...] = jnp.ones_like(ones)
    turn(0)
    to_own(pair)
    norm(0)
    project(0, chunk_of(0))

    pl.semaphore_wait(barrier, 128)

    for u in range(2):
        @pl.loop(0, CHUNKS)
        def _(step):
            g = chunk_of(step)
            if u == 0:
                @pl.when(step > 0)
                def _():
                    project(u, g)
            else:
                project(u, g)

            def post(e, h, mine):
                if u == 0:
                    slot = lr0.at[:, :, xhi, r, six, :]
                else:
                    slot = lr1.at[:, pl.ds(xhi * 3, 3), r, six, :]
                send(
                    b.at[e * 2 + h, :, :, six, :], slot,
                    lr_send.at[u], lr_recv.at[u], (e, h * 2 + c), mine,
                )

            chips(g, step == 3, post)

        if u == 0:
            swap = pltpu.make_async_remote_copy(
                pair.at[pl.ds((1 - c) * IL, IL)], zin.at[...], x_send.at[0], x_recv.at[0],
                device_id=partner, device_id_type=MESH,
            )
            swap.start()
            turn(1)
            k_id = lax.broadcasted_iota(jnp.int32, (512, 384), 0)
            i_id = lax.broadcasted_iota(jnp.int32, (512, 384), 1)
            row = k_id % 256 // 8 * 12 + k_id // 256 * IL + k_id % 8
            sel[...] = jnp.where((k_id % 8 < IL) & (row == i_id), 1.0, 0.0).astype(BF16)
            k_id = lax.broadcasted_iota(jnp.int32, (384, 512), 1)
            i_id = lax.broadcasted_iota(jnp.int32, (384, 512), 0)
            row = k_id % 256 // 8 * 12 + k_id // 256 * IL + k_id % 8
            selt[...] = jnp.where((k_id % 8 < IL) & (row == i_id), 1.0, 0.0).astype(BF16)
            swap.wait()
            zbuf[:, mine_at, :] = pair[pl.ds(c * IL, IL)]
            zbuf[:, other_at, :] = zin[...]
        else:
            swap = pltpu.make_async_remote_copy(
                zbuf.at[:, other_at, :], zown.at[pl.ds(c * IL, IL)], x_send.at[1], x_recv.at[1],
                device_id=partner, device_id_type=MESH,
            )
            swap.start()
            zown[pl.ds(c * IL, IL)] = zbuf[:, mine_at, :]
            swap.wait()
            to_own(zown)
        norm(u)
        gates(u)

        whole = b.at[:, :, :, six, :]
        most = b.at[pl.ds(0, CH - 1), :, :, six, :]
        pltpu.make_async_copy(whole, whole, lr_recv.at[u]).wait()
        pltpu.make_async_copy(most, most, lr_send.at[u]).wait()

        if u == 0:
            xs, xp = xs0, xp0
            for s in range(2):
                t0, t1 = lr0[s, 2, 0].reshape(512, 128), lr0[s, 2, 1].reshape(512, 128)
                tl[s, 0] = halves(t0[:, :64], t1[:, :64])
                tl[s, 1] = halves(t0[:, 64:], t1[:, 64:])
            for half in range(2):
                at = slice(half * 32, half * 32 + 32)
                parts = [
                    jnp.concatenate(
                        [lr0[1, d, 0, at].reshape(256, 128), lr0[1, d, 1, at].reshape(256, 128),
                         tl[1, d, half * 256 : half * 256 + 256]], axis=1,
                    )
                    for d in range(2)
                ]
                rc[384 * half : 384 * half + 384, :] = dot(
                    selt[...], jnp.concatenate(parts, axis=0), NN
                ).astype(BF16)

            def product(d, n):
                at = pl.ds(n * 16, 16)
                left = [lr0[0, d, h, at].reshape(128, 128) for h in range(2)]
                left.append(tl[0, d, pl.ds(pl.multiple_of(n * 128, 128), 128), :])
                return dot(jnp.concatenate(left, axis=1), rc[...], NT)
        else:
            xs, xp = xs1, xp1
            for half in range(2):
                part = [lr1[0, half * 3 + k].reshape(512, 128) for k in range(3)]
                turned = dot(sel[...], jnp.concatenate(part, axis=1), NT).astype(BF16)
                for d in range(2):
                    lt[d, half * 256 : half * 256 + 256] = turned[d * 256 : d * 256 + 256]
            t0, t1 = lr1[1, 1].reshape(512, 128), lr1[1, 4].reshape(512, 128)
            tl[0, 0] = halves(t0[:, :64], t1[:, :64])
            tl[0, 1] = halves(t0[:, 64:], t1[:, 64:])

            def product(d, n):
                at = pl.ds(pl.multiple_of(n * 128, 128), 128)
                left = jnp.concatenate([lt[0, at], lt[1, at]], axis=0)
                right = [lr1[1, h * 3 + 2 * d].reshape(512, 128) for h in range(2)]
                return dot(left, jnp.concatenate(right + [tl[0, d]], axis=1), NN)

        def give(n):
            return pltpu.make_async_remote_copy(
                xs.at[n], xp.at[n], p_send.at[u, n], p_recv.at[u, n],
                device_id=partner, device_id_type=MESH,
            )

        @pl.loop(0, CHUNKS)
        def _(step):
            n = chunk_of(step)
            xs[n] = product(1 - c, n).astype(BF16)
            give(n).start()

        @pl.loop(0, CHUNKS)
        def _(step):
            n = chunk_of(step)
            p = product(c, n)
            give(n).wait_recv()
            p = p + xp[n].astype(F32)
            at = pl.ds(n * 16, 16)
            if u == 0:
                for h in range(2):
                    for k in range(3):
                        tile = p[:, (h * 3 + k) * 128 : (h * 3 + k + 1) * 128]
                        ts[at, h, k] = tile.reshape(16, 8, 128).astype(BF16)
            else:
                low, high = p[0:128], p[128:256]
                for h in range(2):
                    cols = slice(256 + h * 64, 320 + h * 64)
                    ts[at, h, 0] = low[:, h * 128 : h * 128 + 128].reshape(16, 8, 128).astype(BF16)
                    ts[at, h, 1] = high[:, h * 128 : h * 128 + 128].reshape(16, 8, 128).astype(BF16)
                    tile = halves(low[:, cols], high[:, cols])
                    ts[at, h, 2] = tile.reshape(16, 8, 128).astype(BF16)

            def post(e, h, mine):
                send(
                    ts.at[e, h, :, six, :], tri.at[u, :, chip, six, :],
                    t_send.at[u], t_recv.at[u], (e, h * 2 + c), mine,
                )

            chips(n, step == 3, post)

        for n in range(CHUNKS):
            give(n).wait_send()
        whole = tri.at[u, :, :, six, :]
        most = tri.at[u, :, pl.ds(0, CH - 1), six, :]
        pltpu.make_async_copy(whole, whole, t_recv.at[u]).wait()

        @pl.loop(0, 3)
        def _(k):
            tf[...] = tri[u, k].astype(F32).reshape(CH * 8, 128)
            at = pl.ds(pl.multiple_of(k * 128, 128), 128)
            for i in range(IL):
                val = tf[pl.ds(i, CH, stride=8), :]
                shifted = val - jnp.mean(val, axis=0, keepdims=True)
                spread = jnp.mean(shifted * shifted, axis=0, keepdims=True)
                normed = (shifted * lax.rsqrt(spread + 1e-05) * gcol[u]).astype(BF16)
                term = dot(normed, w_out[u], TN) * gate[i, at, :]
                zbuf[i, at, :] = (zbuf[i, at, :].astype(F32) + term).astype(BF16)

        pltpu.make_async_copy(most, most, t_send.at[u]).wait()
        if u == 0:
            norm(1)

    @pl.loop(0, IL)
    def _(i):
        out_ref[i, main_at] = zbuf[i, 0:128]
        out_ref[IL + i, main_at] = zbuf[i, 128:256]
        out_ref[i, tail_at] = zbuf[i, 256:320]
        out_ref[IL + i, tail_at] = zbuf[i, 320:384]


def on_device(pair, residue_mask, in_gain, w_in, out_gain, w_out):
    hbm = pl.BlockSpec(memory_space=pl.ANY)
    dma = pltpu.SemaphoreType.DMA
    return pl.pallas_call(
        kernel,
        out_shape=jax.ShapeDtypeStruct(pair.shape, BF16),
        in_specs=[hbm] * 7,
        out_specs=pl.BlockSpec(memory_space=pltpu.VMEM),
        scratch_shapes=[
            pltpu.VMEM(pair.shape, BF16),
            pltpu.SMEM((768,), jnp.int32),
            pltpu.VMEM((6, 128), jnp.int32),
            pltpu.VMEM(in_gain.shape, F32),
            pltpu.VMEM(w_in.shape, BF16),
            pltpu.VMEM(out_gain.shape, F32),
            pltpu.VMEM(w_out.shape, BF16),
            pltpu.VMEM((IL, 192, CH), BF16),
            pltpu.VMEM((IL, 384, CH), BF16),
            pltpu.VMEM((2 * IL, 192, CH), BF16),
            pltpu.VMEM((IL, 384, CH), BF16),
            pltpu.VMEM((IL, 384, CH), F32),
            pltpu.VMEM((2, CHUNKS, 4 * CW, CH), BF16),
            pltpu.VMEM((2, 3, CW * 8, 128), F32),
            pltpu.VMEM((CH, 2, 3, 8, 128), BF16),
            pltpu.VMEM((2, 3, 2, 64, 8, 128), BF16),
            pltpu.VMEM((2, 6, 64, 8, 128), BF16),
            pltpu.VMEM((768, 384), BF16),
            pltpu.VMEM((2, 512, 512), BF16),
            pltpu.VMEM((2, 2, 512, 128), BF16),
            pltpu.VMEM((512, 384), BF16),
            pltpu.VMEM((384, 512), BF16),
            pltpu.VMEM((4, 128, 768), BF16),
            pltpu.VMEM((4, 128, 768), BF16),
            pltpu.VMEM((4, 256, 384), BF16),
            pltpu.VMEM((4, 256, 384), BF16),
            pltpu.VMEM((64, 2, 3, 8, 128), BF16),
            pltpu.VMEM((2, 3, CH, 8, 128), BF16),
            pltpu.VMEM((CH * 8, 128), F32),
            pltpu.VMEM((2, CH, 128), F32),
            pltpu.VMEM((2, 8, 384), F32),
            pltpu.VMEM((CH, 128), BF16),
            dma((7,)), dma((2,)), dma((2,)), dma((2, 4)), dma((2, 4)),
            dma((2,)), dma((2,)), dma((2,)), dma((2,)),
        ],
        compiler_params=pltpu.CompilerParams(
            collective_id=0, has_side_effects=True, vmem_limit_bytes=48 * 2**20
        ),
        name="triangle",
    )(pair, residue_mask, residue_mask.reshape(6, 128), in_gain, w_in, out_gain, w_out)


def solution(mesh):
    placed = (P("row", "col", None), P(), P(), P(), P(), P())
    return jax.shard_map(
        on_device, mesh=mesh, in_specs=placed, out_specs=P("row", "col", None), check_vma=False
    )
```

```python
import jax
import jax.numpy as jnp
from jax import lax
from jax.experimental import pallas as pl
from jax.experimental.pallas import tpu as pltpu
from jax.sharding import PartitionSpec as P

MESH = pl.DeviceIdType.MESH
F32 = jnp.float32
BF16 = jnp.bfloat16
CH = 128
IL = 6
CHUNKS = 4
CW = CH // CHUNKS
NT = (((1,), (1,)), ((), ()))
NN = (((1,), (0,)), ((), ()))
TN = (((0,), (0,)), ((), ()))


def dot(a, b, dims):
    return lax.dot_general(a, b, dims, preferred_element_type=F32)


def sigmoid(v):
    return 0.5 * jnp.tanh(0.5 * v) + 0.5


def halves(a, b):
    return jnp.concatenate([a, b], axis=1)


def kernel(
    pair_hbm, mask_hbm, mask6_hbm, in_gain_hbm, w_in_hbm, out_gain_hbm, w_out_hbm, out_ref,
    pair, mask_s, mask_v, in_gain, w_in, out_gain, w_out,
    zin, zbuf, zown, xn, gate, wt, bf, b, lr0, lr1, rc, lt, tl, sel, selt, xs0, xp0, xs1, xp1,
    ts, tri, tf, gcol, pm, ones,
    in_sem, x_send, x_recv, p_send, p_recv, lr_send, lr_recv, t_send, t_recv,
):
    r = lax.axis_index("row")
    q = lax.axis_index("col")
    xhi = q // 2
    c = q % 2
    partner = (r, xhi * 2 + 1 - c)
    chip = r * 2 + xhi
    main_at = pl.ds(pl.multiple_of(c * 64, 64), 128)
    tail_at = pl.ds(pl.multiple_of((1 - c) * 128, 128), 64)
    mine_at = pl.ds(pl.multiple_of(c * 192, 64), 192)
    other_at = pl.ds(pl.multiple_of((1 - c) * 192, 64), 192)
    six = pl.ds(0, IL)

    loads = [
        pltpu.make_async_copy(src, dst, in_sem.at[n])
        for n, (src, dst) in enumerate(
            (
                (pair_hbm, pair), (mask_hbm, mask_s), (mask6_hbm, mask_v), (in_gain_hbm, in_gain),
                (w_in_hbm, w_in), (out_gain_hbm, out_gain), (w_out_hbm, w_out),
            )
        )
    ]
    for load in loads:
        load.start()

    lr0[1] = jnp.zeros(lr0.shape[1:], BF16)

    bits = [r // 2**k % 2 for k in range(4)]

    def chunk_of(step):
        zh = r // 16
        b1, b0 = 1 - step // 2, 1 - step % 2
        return 2 * ((zh // 2 + b1) % 2) + (zh % 2 + b0) % 2

    def chips(g, z0, y0, step, visit):
        mine = (step == CHUNKS - 1) & (bits[3] == z0) & (bits[0] == y0)
        for low in range(7, -1, -1):
            e = g * 16 + 8 * z0 + y0
            e = e + 4 * (1 - bits[2] if low & 4 else bits[2])
            e = e + 2 * (1 - bits[1] if low & 2 else bits[1])
            h = 1 - xhi if low & 1 else xhi
            visit(e, h, low == 0 and mine)

    quarters = ((0, 0), (1, 1), (0, 1), (1, 0))

    barrier = pltpu.get_barrier_semaphore()
    pl.semaphore_signal(barrier, inc=1, device_id=partner, device_id_type=MESH)

    @pl.loop(0, CHUNKS)
    def _(step):
        def greet(e, h, mine):
            def signal():
                pl.semaphore_signal(barrier, inc=1, device_id=(e, h * 2 + c), device_id_type=MESH)

            if mine is False:
                signal()
            else:
                pl.when(jnp.logical_not(mine))(signal)

        for quarter in quarters:
            chips(chunk_of(step), *quarter, step, greet)

    for load in loads:
        load.wait()

    def turn(u):
        for v in range(4):
            turned = w_in[u, v].astype(F32).T.astype(BF16)
            for g in range(CHUNKS):
                wt[u, g, v * CW : (v + 1) * CW, :] = turned[g * CW : (g + 1) * CW]
        gcol[u] = jnp.broadcast_to(out_gain[u : u + 1, :], (CH, CH)).T

    def norm(u):
        @pl.loop(0, IL, unroll=6)
        def _(i):
            val = zbuf[i]
            shifted = val.astype(F32) - dot(val, ones[...], NN) * (1.0 / CH)
            spread = dot((shifted * shifted).astype(BF16), ones[...], NN) * (1.0 / CH)
            xn[i] = (shifted * lax.rsqrt(spread + 1e-05) * in_gain[u : u + 1, :]).astype(BF16)

    def gates(u):
        @pl.loop(0, IL, unroll=6)
        def _(i):
            gate[i] = sigmoid(dot(xn[i], w_in[u, 4], NN))

    def to_own(src):
        @pl.loop(0, IL)
        def _(i):
            zbuf[i, 0:128] = src[i, main_at]
            zbuf[i, 128:256] = src[IL + i, main_at]
            zbuf[i, 256:320] = src[i, tail_at]
            zbuf[i, 320:384] = src[IL + i, tail_at]

    def project(u, g):
        @pl.loop(0, IL, unroll=6)
        def _(i):
            o = dot(wt[u, g], xn[i], NT)
            mask = pm[u, pl.ds(i, 1), :]
            for s in range(2):
                side = sigmoid(o[2 * s * CW : (2 * s + 1) * CW])
                side = side * o[(2 * s + 1) * CW : (2 * s + 2) * CW] * mask
                for k in range(3):
                    bf[s, k, pl.ds(i, CW, stride=8), :] = side[:, k * 128 : (k + 1) * 128]

        for s in range(2):
            for k in range(3):
                b[pl.ds(g * CW, CW), s, k] = bf[s, k].reshape(CW, 8, 128).astype(BF16)

    def send(src, dst, send_sem, recv_sem, to, mine):
        def remote():
            pltpu.make_async_remote_copy(
                src, dst, send_sem, recv_sem, device_id=to, device_id_type=MESH
            ).start()

        if mine is False:
            remote()
        else:
            pl.when(jnp.logical_not(mine))(remote)

            @pl.when(mine)
            def _():
                pltpu.make_async_copy(src, dst, recv_sem).start()

    lane = lax.broadcasted_iota(jnp.int32, (1, 128), 1)
    row_mask = [mask_s[r * 12 + i].astype(F32) for i in range(2 * IL)]
    main = mask_v[pl.ds(xhi * 3 + 2 * c, 1), :].astype(F32)
    tile = mask_v[pl.ds(xhi * 3 + 1, 1), :].astype(F32)
    swapped = halves(tile[:, 64:], tile[:, :64])
    tail = jnp.where((lane < 64) == (c == 0), tile, swapped)
    for i in range(IL):
        pm[0, i : i + 1, 0:128] = main * row_mask[i]
        pm[0, i : i + 1, 128:256] = main * row_mask[IL + i]
        pm[0, i : i + 1, 256:384] = tail * jnp.where(lane < 64, row_mask[i], row_mask[IL + i])
        for k in range(3):
            cols = mask_v[pl.ds(xhi * 3 + k, 1), :].astype(F32)
            pm[1, i : i + 1, k * 128 : (k + 1) * 128] = cols * jnp.where(
                c == 0, row_mask[i], row_mask[IL + i]
            )

    ones[...] = jnp.ones_like(ones)
    turn(0)
    to_own(pair)
    norm(0)
    project(0, chunk_of(0))

    pl.semaphore_wait(barrier, 128)

    for u in range(2):
        b_six = b.at[:, :, :, six, :]
        for k in range(4):
            def post(e, h, mine):
                if u == 0:
                    slot = lr0.at[:, :, xhi, r, six, :]
                else:
                    slot = lr1.at[:, pl.ds(xhi * 3, 3), r, six, :]
                send(
                    b.at[e * 2 + h, :, :, six, :], slot,
                    lr_send.at[u], lr_recv.at[u], (e, h * 2 + c), mine,
                )

            @pl.loop(0, CHUNKS)
            def _(step):
                g = chunk_of(step)
                if k == 0 and u == 0:
                    pl.when(step > 0)(lambda: project(u, g))
                elif k == 0:
                    project(u, g)
                chips(g, *quarters[k], step, post)

        if u == 0:
            swap = pltpu.make_async_remote_copy(
                pair.at[pl.ds((1 - c) * IL, IL)], zin.at[...], x_send.at[0], x_recv.at[0],
                device_id=partner, device_id_type=MESH,
            )
            swap.start()
            lr1[...] = jnp.zeros_like(lr1)
            turn(1)
            k_id = lax.broadcasted_iota(jnp.int32, (512, 384), 0)
            i_id = lax.broadcasted_iota(jnp.int32, (512, 384), 1)
            row = k_id % 256 // 8 * 12 + k_id // 256 * IL + k_id % 8
            sel[...] = jnp.where((k_id % 8 < IL) & (row == i_id), 1.0, 0.0).astype(BF16)
            k_id = lax.broadcasted_iota(jnp.int32, (384, 512), 1)
            i_id = lax.broadcasted_iota(jnp.int32, (384, 512), 0)
            row = k_id % 256 // 8 * 12 + k_id // 256 * IL + k_id % 8
            selt[...] = jnp.where((k_id % 8 < IL) & (row == i_id), 1.0, 0.0).astype(BF16)
            swap.wait()
            zbuf[:, mine_at, :] = pair[pl.ds(c * IL, IL)]
            zbuf[:, other_at, :] = zin[...]
        else:
            swap = pltpu.make_async_remote_copy(
                zbuf.at[:, other_at, :], zown.at[pl.ds(c * IL, IL)], x_send.at[1], x_recv.at[1],
                device_id=partner, device_id_type=MESH,
            )
            swap.start()
            zown[pl.ds(c * IL, IL)] = zbuf[:, mine_at, :]
            swap.wait()
            to_own(zown)
        norm(u)
        gates(u)

        pltpu.make_async_copy(b_six, b_six, lr_recv.at[u]).wait()
        most = b.at[pl.ds(0, CH - 1), :, :, six, :]
        pltpu.make_async_copy(most, most, lr_send.at[u]).wait()

        if u == 0:
            xs, xp = xs0, xp0
            for s in range(2):
                t0, t1 = lr0[s, 2, 0].reshape(512, 128), lr0[s, 2, 1].reshape(512, 128)
                tl[s, 0] = halves(t0[:, :64], t1[:, :64])
                tl[s, 1] = halves(t0[:, 64:], t1[:, 64:])
            for half in range(2):
                at = slice(half * 32, half * 32 + 32)
                parts = [
                    jnp.concatenate(
                        [lr0[1, d, 0, at].reshape(256, 128), lr0[1, d, 1, at].reshape(256, 128),
                         tl[1, d, half * 256 : half * 256 + 256]], axis=1,
                    )
                    for d in range(2)
                ]
                rc[384 * half : 384 * half + 384, :] = dot(
                    selt[...], jnp.concatenate(parts, axis=0), NN
                ).astype(BF16)

            def product(d, n):
                at = pl.ds(n * 16, 16)
                left = [lr0[0, d, h, at].reshape(128, 128) for h in range(2)]
                left.append(tl[0, d, pl.ds(pl.multiple_of(n * 128, 128), 128), :])
                return dot(jnp.concatenate(left, axis=1), rc[...], NT)
        else:
            xs, xp = xs1, xp1
            for half in range(2):
                part = [lr1[0, half * 3 + k].reshape(512, 128) for k in range(3)]
                turned = dot(sel[...], jnp.concatenate(part, axis=1), NT).astype(BF16)
                for d in range(2):
                    lt[d, half * 256 : half * 256 + 256] = turned[d * 256 : d * 256 + 256]
            t0, t1 = lr1[1, 1].reshape(512, 128), lr1[1, 4].reshape(512, 128)
            tl[0, 0] = halves(t0[:, :64], t1[:, :64])
            tl[0, 1] = halves(t0[:, 64:], t1[:, 64:])

            def product(d, n):
                at = pl.ds(pl.multiple_of(n * 128, 128), 128)
                left = jnp.concatenate([lt[0, at], lt[1, at]], axis=0)
                right = [lr1[1, h * 3 + 2 * d].reshape(512, 128) for h in range(2)]
                return dot(left, jnp.concatenate(right + [tl[0, d]], axis=1), NN)

        def give(n):
            return pltpu.make_async_remote_copy(
                xs.at[n], xp.at[n], p_send.at[u, n], p_recv.at[u, n],
                device_id=partner, device_id_type=MESH,
            )

        @pl.loop(0, CHUNKS, unroll=4)
        def _(step):
            n = chunk_of(step)
            xs[n] = product(1 - c, n).astype(BF16)
            give(n).start()

        def back(e, h, mine):
            send(
                ts.at[e, h, :, six, :], tri.at[u, :, chip, six, :],
                t_send.at[u], t_recv.at[u], (e, h * 2 + c), mine,
            )

        @pl.loop(0, CHUNKS)
        def _(step):
            n = chunk_of(step)
            p = product(c, n)
            give(n).wait_recv()
            p = p + xp[n].astype(F32)
            at = pl.ds(n * 16, 16)
            if u == 0:
                for h in range(2):
                    for k in range(3):
                        tile = p[:, (h * 3 + k) * 128 : (h * 3 + k + 1) * 128]
                        ts[at, h, k] = tile.reshape(16, 8, 128).astype(BF16)
            else:
                low, high = p[0:128], p[128:256]
                for h in range(2):
                    cols = slice(256 + h * 64, 320 + h * 64)
                    ts[at, h, 0] = low[:, h * 128 : h * 128 + 128].reshape(16, 8, 128).astype(BF16)
                    ts[at, h, 1] = high[:, h * 128 : h * 128 + 128].reshape(16, 8, 128).astype(BF16)
                    tile = halves(low[:, cols], high[:, cols])
                    ts[at, h, 2] = tile.reshape(16, 8, 128).astype(BF16)

            chips(n, *quarters[0], step, back)

        for k in range(1, 4):
            @pl.loop(0, CHUNKS)
            def _(step):
                chips(chunk_of(step), *quarters[k], step, back)

        for n in range(CHUNKS):
            give(n).wait_send()
        whole = tri.at[u, :, :, six, :]
        pltpu.make_async_copy(whole, whole, t_recv.at[u]).wait()

        @pl.loop(0, 3, unroll=3)
        def _(k):
            tf[...] = tri[u, k].astype(F32).reshape(CH * 8, 128)
            at = pl.ds(pl.multiple_of(k * 128, 128), 128)
            for i in range(IL):
                val = tf[pl.ds(i, CH, stride=8), :]
                shifted = val - jnp.mean(val, axis=0, keepdims=True)
                spread = jnp.mean(shifted * shifted, axis=0, keepdims=True)
                normed = (shifted * lax.rsqrt(spread + 1e-05) * gcol[u]).astype(BF16)
                term = dot(normed, w_out[u], TN) * gate[i, at, :]
                zbuf[i, at, :] = (zbuf[i, at, :].astype(F32) + term).astype(BF16)

        most = tri.at[u, :, pl.ds(0, CH - 1), six, :]
        pltpu.make_async_copy(most, most, t_send.at[u]).wait()
        if u == 0:
            norm(1)

    @pl.loop(0, IL)
    def _(i):
        out_ref[i, main_at] = zbuf[i, 0:128]
        out_ref[IL + i, main_at] = zbuf[i, 128:256]
        out_ref[i, tail_at] = zbuf[i, 256:320]
        out_ref[IL + i, tail_at] = zbuf[i, 320:384]


def on_device(pair, residue_mask, in_gain, w_in, out_gain, w_out):
    hbm = pl.BlockSpec(memory_space=pl.ANY)
    dma = pltpu.SemaphoreType.DMA
    return pl.pallas_call(
        kernel,
        out_shape=jax.ShapeDtypeStruct(pair.shape, BF16),
        in_specs=[hbm] * 7,
        out_specs=pl.BlockSpec(memory_space=pltpu.VMEM),
        scratch_shapes=[
            pltpu.VMEM(pair.shape, BF16),
            pltpu.SMEM((768,), jnp.int32),
            pltpu.VMEM((6, 128), jnp.int32),
            pltpu.VMEM(in_gain.shape, F32),
            pltpu.VMEM(w_in.shape, BF16),
            pltpu.VMEM(out_gain.shape, F32),
            pltpu.VMEM(w_out.shape, BF16),
            pltpu.VMEM((IL, 192, CH), BF16),
            pltpu.VMEM((IL, 384, CH), BF16),
            pltpu.VMEM((2 * IL, 192, CH), BF16),
            pltpu.VMEM((IL, 384, CH), BF16),
            pltpu.VMEM((IL, 384, CH), F32),
            pltpu.VMEM((2, CHUNKS, 4 * CW, CH), BF16),
            pltpu.VMEM((2, 3, CW * 8, 128), F32),
            pltpu.VMEM((CH, 2, 3, 8, 128), BF16),
            pltpu.VMEM((2, 3, 2, 64, 8, 128), BF16),
            pltpu.VMEM((2, 6, 64, 8, 128), BF16),
            pltpu.VMEM((768, 384), BF16),
            pltpu.VMEM((2, 512, 512), BF16),
            pltpu.VMEM((2, 2, 512, 128), BF16),
            pltpu.VMEM((512, 384), BF16),
            pltpu.VMEM((384, 512), BF16),
            pltpu.VMEM((4, 128, 768), BF16),
            pltpu.VMEM((4, 128, 768), BF16),
            pltpu.VMEM((4, 256, 384), BF16),
            pltpu.VMEM((4, 256, 384), BF16),
            pltpu.VMEM((64, 2, 3, 8, 128), BF16),
            pltpu.VMEM((2, 3, CH, 8, 128), BF16),
            pltpu.VMEM((CH * 8, 128), F32),
            pltpu.VMEM((2, CH, 128), F32),
            pltpu.VMEM((2, 8, 384), F32),
            pltpu.VMEM((CH, 128), BF16),
            dma((7,)), dma((2,)), dma((2,)), dma((2, 4)), dma((2, 4)),
            dma((2,)), dma((2,)), dma((2,)), dma((2,)),
        ],
        compiler_params=pltpu.CompilerParams(
            collective_id=0, has_side_effects=True, vmem_limit_bytes=62 * 2**20
        ),
        name="triangle",
    )(pair, residue_mask, residue_mask.reshape(6, 128), in_gain, w_in, out_gain, w_out)


def solution(mesh):
    placed = (P("row", "col", None), P(), P(), P(), P(), P())
    return jax.shard_map(
        on_device, mesh=mesh, in_specs=placed, out_specs=P("row", "col", None), check_vma=False
    )
```

```python
import jax
import jax.numpy as jnp
from jax import lax
from jax.experimental import pallas as pl
from jax.experimental.pallas import tpu as pltpu
from jax.sharding import PartitionSpec as P

MESH = pl.DeviceIdType.MESH
F32 = jnp.float32
BF16 = jnp.bfloat16
CH = 128
IL = 6
CHUNKS = 4
CW = CH // CHUNKS
ORDER = (2, 3, 1, 0)
FIXED = ("z0", "y0")
GROUPS = ((0, 0), (1, 1), (0, 1), (1, 0))
FREE = ("xhi", "y0", "y1", "xlo", "z0")
STAGES = (((0, 1), (1, 2)), ((0, 3),))
NT = (((1,), (1,)), ((), ()))
NN = (((1,), (0,)), ((), ()))
TN = (((0,), (0,)), ((), ()))


def dot(a, b, dims):
    return lax.dot_general(a, b, dims, preferred_element_type=F32)


def sigmoid(v):
    return 0.5 * jnp.tanh(0.5 * v) + 0.5


def halves(a, b):
    return jnp.concatenate([a, b], axis=1)


def kernel(
    pair_hbm, mask_hbm, mask6_hbm, in_gain_hbm, w_in_hbm, out_gain_hbm, w_out_hbm, out_ref,
    pair, mask_s, mask_v, in_gain, w_in, out_gain, w_out,
    zin, zbuf, zown, xn, gate, wt, bf, b, lr0, lr1, rc, lt, tl, sel, selt, xs0, xp0, xs1, xp1,
    ts, tri, tf, gcol, pm, ones,
    in_sem, x_send, x_recv, p_send, p_recv, lr_send, lr_recv, t_send, t_recv,
):
    r = lax.axis_index("row")
    q = lax.axis_index("col")
    xhi = q // 2
    c = q % 2
    partner = (r, xhi * 2 + 1 - c)
    chip = r * 2 + xhi
    main_at = pl.ds(pl.multiple_of(c * 64, 64), 128)
    tail_at = pl.ds(pl.multiple_of((1 - c) * 128, 128), 64)
    mine_at = pl.ds(pl.multiple_of(c * 192, 64), 192)
    other_at = pl.ds(pl.multiple_of((1 - c) * 192, 64), 192)
    six = pl.ds(0, IL)

    loads = [
        pltpu.make_async_copy(src, dst, in_sem.at[n])
        for n, (src, dst) in enumerate(
            (
                (pair_hbm, pair), (mask_hbm, mask_s), (mask6_hbm, mask_v), (in_gain_hbm, in_gain),
                (w_in_hbm, w_in), (out_gain_hbm, out_gain), (w_out_hbm, w_out),
            )
        )
    ]
    for load in loads:
        load.start()

    lr0[1] = jnp.zeros(lr0.shape[1:], BF16)

    bits = [r // 2**k % 2 for k in range(4)]

    def chunk_of(step):
        zh = r // 16
        flip = ORDER[-1]
        for n in range(CHUNKS - 1):
            flip = flip + jnp.where(step == n, ORDER[n] - ORDER[-1], 0)
        return 2 * ((zh // 2 + flip // 2) % 2) + (zh % 2 + flip % 2) % 2

    place = {"xhi": 1, "y0": 2, "y1": 4, "xlo": 8, "z0": 16}
    here = dict(zip(place, [xhi] + bits))
    free = [name for name in FREE if name not in FIXED]

    def chips(g, group, step, visit):
        mine = step == CHUNKS - 1
        for name, value in zip(FIXED, group):
            mine = mine & (here[name] == value)
        for low in range(2 ** len(free) - 1, -1, -1):
            to = dict(zip(FIXED, group))
            for k, name in enumerate(free):
                to[name] = 1 - here[name] if low >> k & 1 else here[name]
            e = g * 16
            for name in list(place)[1:]:
                e = e + to[name] * (place[name] // 2)
            visit(e, to["xhi"], low == 0 and mine)

    barrier = pltpu.get_barrier_semaphore()
    pl.semaphore_signal(barrier, inc=1, device_id=partner, device_id_type=MESH)

    @pl.loop(0, CHUNKS)
    def _(step):
        def greet(e, h, mine):
            def signal():
                pl.semaphore_signal(barrier, inc=1, device_id=(e, h * 2 + c), device_id_type=MESH)

            if mine is False:
                signal()
            else:
                pl.when(jnp.logical_not(mine))(signal)

        for group in GROUPS:
            chips(chunk_of(step), group, step, greet)

    for load in loads:
        load.wait()

    def turn(u):
        for v in range(4):
            turned = w_in[u, v].astype(F32).T.astype(BF16)
            for g in range(CHUNKS):
                wt[u, g, v * CW : (v + 1) * CW, :] = turned[g * CW : (g + 1) * CW]
        gcol[u] = jnp.broadcast_to(out_gain[u : u + 1, :], (CH, CH)).T

    def norm(u, lo=0, n=3):
        at = pl.ds(lo * 128, n * 128)

        @pl.loop(0, IL, unroll=6)
        def _(i):
            val = zbuf[i, at]
            shifted = val.astype(F32) - dot(val, ones[...], NN) * (1.0 / CH)
            spread = dot((shifted * shifted).astype(BF16), ones[...], NN) * (1.0 / CH)
            xn[i, at] = (shifted * lax.rsqrt(spread + 1e-05) * in_gain[u : u + 1, :]).astype(BF16)

    def gates(u):
        @pl.loop(0, IL, unroll=6)
        def _(i):
            gate[i] = sigmoid(dot(xn[i], w_in[u, 4], NN))

    def to_own(src):
        @pl.loop(0, IL)
        def _(i):
            zbuf[i, 0:128] = src[i, main_at]
            zbuf[i, 128:256] = src[IL + i, main_at]
            zbuf[i, 256:320] = src[i, tail_at]
            zbuf[i, 320:384] = src[IL + i, tail_at]

    def project(u, g, lo, n):
        at = pl.ds(lo * 128, n * 128)

        @pl.loop(0, IL, unroll=6)
        def _(i):
            o = dot(wt[u, g], xn[i, at], NT)
            mask = pm[u, pl.ds(i, 1), at]
            for s in range(2):
                side = sigmoid(o[2 * s * CW : (2 * s + 1) * CW])
                side = side * o[(2 * s + 1) * CW : (2 * s + 2) * CW] * mask
                for k in range(n):
                    bf[s, k, pl.ds(i, CW, stride=8), :] = side[:, k * 128 : (k + 1) * 128]

        for s in range(2):
            for k in range(n):
                b[pl.ds(g * CW, CW), s, lo + k] = bf[s, k].reshape(CW, 8, 128).astype(BF16)

    def send(src, dst, send_sem, recv_sem, to, mine):
        def remote():
            pltpu.make_async_remote_copy(
                src, dst, send_sem, recv_sem, device_id=to, device_id_type=MESH
            ).start()

        if mine is False:
            remote()
        else:
            pl.when(jnp.logical_not(mine))(remote)

            @pl.when(mine)
            def _():
                pltpu.make_async_copy(src, dst, recv_sem).start()

    lane = lax.broadcasted_iota(jnp.int32, (1, 128), 1)
    row_mask = [mask_s[r * 12 + i].astype(F32) for i in range(2 * IL)]
    main = mask_v[pl.ds(xhi * 3 + 2 * c, 1), :].astype(F32)
    tile = mask_v[pl.ds(xhi * 3 + 1, 1), :].astype(F32)
    swapped = halves(tile[:, 64:], tile[:, :64])
    tail = jnp.where((lane < 64) == (c == 0), tile, swapped)
    for i in range(IL):
        pm[0, i : i + 1, 0:128] = main * row_mask[i]
        pm[0, i : i + 1, 128:256] = main * row_mask[IL + i]
        pm[0, i : i + 1, 256:384] = tail * jnp.where(lane < 64, row_mask[i], row_mask[IL + i])
        for k in range(3):
            cols = mask_v[pl.ds(xhi * 3 + k, 1), :].astype(F32)
            pm[1, i : i + 1, k * 128 : (k + 1) * 128] = cols * jnp.where(
                c == 0, row_mask[i], row_mask[IL + i]
            )

    ones[...] = jnp.ones_like(ones)
    turn(0)
    to_own(pair)
    norm(0)
    project(0, chunk_of(0), 0, 3)

    pl.semaphore_wait(barrier, 128)

    def project_send(u, lo, n):
        for k in range(len(GROUPS)):
            def post(e, h, mine):
                if u == 0:
                    slot = lr0.at[:, pl.ds(lo, n), xhi, r, six, :]
                else:
                    slot = lr1.at[:, pl.ds(xhi * 3 + lo, n), r, six, :]
                send(
                    b.at[e * 2 + h, :, pl.ds(lo, n), six, :], slot,
                    lr_send.at[u], lr_recv.at[u], (e, h * 2 + c), mine,
                )

            @pl.loop(0, CHUNKS)
            def _(step):
                g = chunk_of(step)
                if k == 0 and u == 0:
                    pl.when(step > 0)(lambda: project(u, g, lo, n))
                elif k == 0:
                    project(u, g, lo, n)
                chips(g, GROUPS[k], step, post)

    def finish(u, lo, n):
        for k in range(lo, lo + n):
            tf[...] = tri[u, k].astype(F32).reshape(CH * 8, 128)
            at = pl.ds(k * 128, 128)
            for i in range(IL):
                val = tf[pl.ds(i, CH, stride=8), :]
                shifted = val - jnp.mean(val, axis=0, keepdims=True)
                spread = jnp.mean(shifted * shifted, axis=0, keepdims=True)
                normed = (shifted * lax.rsqrt(spread + 1e-05) * gcol[u]).astype(BF16)
                term = dot(normed, w_out[u], TN) * gate[i, at, :]
                zbuf[i, at, :] = (zbuf[i, at, :].astype(F32) + term).astype(BF16)

    for u in range(2):
        if u == 0:
            project_send(0, 0, 3)

        if u == 0:
            swap = pltpu.make_async_remote_copy(
                pair.at[pl.ds((1 - c) * IL, IL)], zin.at[...], x_send.at[0], x_recv.at[0],
                device_id=partner, device_id_type=MESH,
            )
            swap.start()
            lr1[...] = jnp.zeros_like(lr1)
            turn(1)
            k_id = lax.broadcasted_iota(jnp.int32, (512, 384), 0)
            i_id = lax.broadcasted_iota(jnp.int32, (512, 384), 1)
            row = k_id % 256 // 8 * 12 + k_id // 256 * IL + k_id % 8
            sel[...] = jnp.where((k_id % 8 < IL) & (row == i_id), 1.0, 0.0).astype(BF16)
            k_id = lax.broadcasted_iota(jnp.int32, (384, 512), 1)
            i_id = lax.broadcasted_iota(jnp.int32, (384, 512), 0)
            row = k_id % 256 // 8 * 12 + k_id // 256 * IL + k_id % 8
            selt[...] = jnp.where((k_id % 8 < IL) & (row == i_id), 1.0, 0.0).astype(BF16)
            swap.wait()
            zbuf[:, mine_at, :] = pair[pl.ds(c * IL, IL)]
            zbuf[:, other_at, :] = zin[...]
        else:
            swap = pltpu.make_async_remote_copy(
                zbuf.at[:, other_at, :], zown.at[pl.ds(c * IL, IL)], x_send.at[1], x_recv.at[1],
                device_id=partner, device_id_type=MESH,
            )
            swap.start()
            zown[pl.ds(c * IL, IL)] = zbuf[:, mine_at, :]
            swap.wait()
            to_own(zown)
        norm(u)
        gates(u)

        b_six = b.at[:, :, :, six, :]
        pltpu.make_async_copy(b_six, b_six, lr_recv.at[u]).wait()
        most = b.at[pl.ds(0, CH - 1), :, :, six, :]
        pltpu.make_async_copy(most, most, lr_send.at[u]).wait()

        if u == 0:
            xs, xp = xs0, xp0
            for s in range(2):
                t0, t1 = lr0[s, 2, 0].reshape(512, 128), lr0[s, 2, 1].reshape(512, 128)
                tl[s, 0] = halves(t0[:, :64], t1[:, :64])
                tl[s, 1] = halves(t0[:, 64:], t1[:, 64:])
            for half in range(2):
                at = slice(half * 32, half * 32 + 32)
                parts = [
                    jnp.concatenate(
                        [lr0[1, d, 0, at].reshape(256, 128), lr0[1, d, 1, at].reshape(256, 128),
                         tl[1, d, half * 256 : half * 256 + 256]], axis=1,
                    )
                    for d in range(2)
                ]
                rc[384 * half : 384 * half + 384, :] = dot(
                    selt[...], jnp.concatenate(parts, axis=0), NN
                ).astype(BF16)

            def product(d, n):
                at = pl.ds(n * 16, 16)
                left = [lr0[0, d, h, at].reshape(128, 128) for h in range(2)]
                left.append(tl[0, d, pl.ds(pl.multiple_of(n * 128, 128), 128), :])
                return dot(jnp.concatenate(left, axis=1), rc[...], NT)
        else:
            xs, xp = xs1, xp1
            for half in range(2):
                part = [lr1[0, half * 3 + k].reshape(512, 128) for k in range(3)]
                turned = dot(sel[...], jnp.concatenate(part, axis=1), NT).astype(BF16)
                for d in range(2):
                    lt[d, half * 256 : half * 256 + 256] = turned[d * 256 : d * 256 + 256]
            t0, t1 = lr1[1, 1].reshape(512, 128), lr1[1, 4].reshape(512, 128)
            tl[0, 0] = halves(t0[:, :64], t1[:, :64])
            tl[0, 1] = halves(t0[:, 64:], t1[:, 64:])

            def product(d, n):
                at = pl.ds(pl.multiple_of(n * 128, 128), 128)
                left = jnp.concatenate([lt[0, at], lt[1, at]], axis=0)
                right = [lr1[1, h * 3 + 2 * d].reshape(512, 128) for h in range(2)]
                return dot(left, jnp.concatenate(right + [tl[0, d]], axis=1), NN)

        def give(n):
            return pltpu.make_async_remote_copy(
                xs.at[n], xp.at[n], p_send.at[u, n], p_recv.at[u, n],
                device_id=partner, device_id_type=MESH,
            )

        @pl.loop(0, CHUNKS, unroll=4)
        def _(step):
            n = chunk_of(step)
            xs[n] = product(1 - c, n).astype(BF16)
            give(n).start()

        def back(stage):
            lo, n = STAGES[u][stage]

            def post(e, h, mine):
                send(
                    ts.at[e, h, pl.ds(lo, n), six, :], tri.at[u, pl.ds(lo, n), chip, six, :],
                    t_send.at[u], t_recv.at[u, stage], (e, h * 2 + c), mine,
                )

            return post

        @pl.loop(0, CHUNKS)
        def _(step):
            n = chunk_of(step)
            p = product(c, n)
            give(n).wait_recv()
            p = p + xp[n].astype(F32)
            at = pl.ds(n * 16, 16)
            if u == 0:
                for h in range(2):
                    for k in range(3):
                        tile = p[:, (h * 3 + k) * 128 : (h * 3 + k + 1) * 128]
                        ts[at, h, k] = tile.reshape(16, 8, 128).astype(BF16)
            else:
                low, high = p[0:128], p[128:256]
                for h in range(2):
                    cols = slice(256 + h * 64, 320 + h * 64)
                    ts[at, h, 0] = low[:, h * 128 : h * 128 + 128].reshape(16, 8, 128).astype(BF16)
                    ts[at, h, 1] = high[:, h * 128 : h * 128 + 128].reshape(16, 8, 128).astype(BF16)
                    tile = halves(low[:, cols], high[:, cols])
                    ts[at, h, 2] = tile.reshape(16, 8, 128).astype(BF16)

            chips(n, GROUPS[0], step, back(0))

        for stage in range(len(STAGES[u])):
            for k in range(0 if stage else 1, len(GROUPS)):
                @pl.loop(0, CHUNKS)
                def _(step):
                    chips(chunk_of(step), GROUPS[k], step, back(stage))

        for n in range(CHUNKS):
            give(n).wait_send()
        for stage, (lo, n) in enumerate(STAGES[u]):
            part = tri.at[u, pl.ds(lo, n), :, six, :]
            pltpu.make_async_copy(part, part, t_recv.at[u, stage]).wait()
            finish(u, lo, n)
            if u == 0:
                norm(1, lo, n)
                project_send(1, lo, n)
        most = tri.at[u, :, pl.ds(0, CH - 1), six, :]
        pltpu.make_async_copy(most, most, t_send.at[u]).wait()

    @pl.loop(0, IL)
    def _(i):
        out_ref[i, main_at] = zbuf[i, 0:128]
        out_ref[IL + i, main_at] = zbuf[i, 128:256]
        out_ref[i, tail_at] = zbuf[i, 256:320]
        out_ref[IL + i, tail_at] = zbuf[i, 320:384]


def on_device(pair, residue_mask, in_gain, w_in, out_gain, w_out):
    hbm = pl.BlockSpec(memory_space=pl.ANY)
    dma = pltpu.SemaphoreType.DMA
    return pl.pallas_call(
        kernel,
        out_shape=jax.ShapeDtypeStruct(pair.shape, BF16),
        in_specs=[hbm] * 7,
        out_specs=pl.BlockSpec(memory_space=pltpu.VMEM),
        scratch_shapes=[
            pltpu.VMEM(pair.shape, BF16),
            pltpu.SMEM((768,), jnp.int32),
            pltpu.VMEM((6, 128), jnp.int32),
            pltpu.VMEM(in_gain.shape, F32),
            pltpu.VMEM(w_in.shape, BF16),
            pltpu.VMEM(out_gain.shape, F32),
            pltpu.VMEM(w_out.shape, BF16),
            pltpu.VMEM((IL, 192, CH), BF16),
            pltpu.VMEM((IL, 384, CH), BF16),
            pltpu.VMEM((2 * IL, 192, CH), BF16),
            pltpu.VMEM((IL, 384, CH), BF16),
            pltpu.VMEM((IL, 384, CH), F32),
            pltpu.VMEM((2, CHUNKS, 4 * CW, CH), BF16),
            pltpu.VMEM((2, 3, CW * 8, 128), F32),
            pltpu.VMEM((CH, 2, 3, 8, 128), BF16),
            pltpu.VMEM((2, 3, 2, 64, 8, 128), BF16),
            pltpu.VMEM((2, 6, 64, 8, 128), BF16),
            pltpu.VMEM((768, 384), BF16),
            pltpu.VMEM((2, 512, 512), BF16),
            pltpu.VMEM((2, 2, 512, 128), BF16),
            pltpu.VMEM((512, 384), BF16),
            pltpu.VMEM((384, 512), BF16),
            pltpu.VMEM((4, 128, 768), BF16),
            pltpu.VMEM((4, 128, 768), BF16),
            pltpu.VMEM((4, 256, 384), BF16),
            pltpu.VMEM((4, 256, 384), BF16),
            pltpu.VMEM((64, 2, 3, 8, 128), BF16),
            pltpu.VMEM((2, 3, CH, 8, 128), BF16),
            pltpu.VMEM((CH * 8, 128), F32),
            pltpu.VMEM((2, CH, 128), F32),
            pltpu.VMEM((2, 8, 384), F32),
            pltpu.VMEM((CH, 128), BF16),
            dma((7,)), dma((2,)), dma((2,)), dma((2, 4)), dma((2, 4)),
            dma((2,)), dma((2,)), dma((2,)), dma((2, 2)),
        ],
        compiler_params=pltpu.CompilerParams(
            collective_id=0, has_side_effects=True, vmem_limit_bytes=62 * 2**20
        ),
        name="triangle",
    )(pair, residue_mask, residue_mask.reshape(6, 128), in_gain, w_in, out_gain, w_out)


def solution(mesh):
    placed = (P("row", "col", None), P(), P(), P(), P(), P())
    return jax.shard_map(
        on_device, mesh=mesh, in_specs=placed, out_specs=P("row", "col", None), check_vma=False
    )
```

```python
import jax
import jax.numpy as jnp
from jax import lax
from jax.experimental import pallas as pl
from jax.experimental.pallas import tpu as pltpu
from jax.sharding import PartitionSpec as P

MESH = pl.DeviceIdType.MESH
F32 = jnp.float32
BF16 = jnp.bfloat16
CH = 128
IL = 6
CHUNKS = 4
CW = CH // CHUNKS
ORDER = (2, 3, 1, 0)
FIXED = ("z0", "y0")
GROUPS = ((0, 0), (1, 1), (0, 1), (1, 0))
FREE = ("xhi", "y0", "y1", "xlo", "z0")
STAGES = (((0, 1), (1, 2)), ((0, 2), (2, 1)))
NT = (((1,), (1,)), ((), ()))
NN = (((1,), (0,)), ((), ()))
TN = (((0,), (0,)), ((), ()))


def dot(a, b, dims):
    return lax.dot_general(a, b, dims, preferred_element_type=F32)


def sigmoid(v):
    return 0.5 * jnp.tanh(0.5 * v) + 0.5


def halves(a, b):
    return jnp.concatenate([a, b], axis=1)


def kernel(
    pair_hbm, mask_hbm, mask6_hbm, in_gain_hbm, w_in_hbm, out_gain_hbm, w_out_hbm, out_ref,
    pair, mask_s, mask_v, in_gain, w_in, out_gain, w_out,
    zin, zbuf, zown, xn, gate, wt, bf, b, lr0, lr1, rc, lt, tl, sel, selt, xs0, xp0, xs1, xp1, xst, xpt,
    ts, tri, tf, gcol, pm, ones,
    in_sem, x_send, x_recv, p_send, p_recv, lr_send, lr_recv, t_send, t_recv,
):
    r = lax.axis_index("row")
    q = lax.axis_index("col")
    xhi = q // 2
    c = q % 2
    partner = (r, xhi * 2 + 1 - c)
    chip = r * 2 + xhi
    main_at = pl.ds(pl.multiple_of(c * 64, 64), 128)
    tail_at = pl.ds(pl.multiple_of((1 - c) * 128, 128), 64)
    mine_at = pl.ds(pl.multiple_of(c * 192, 64), 192)
    other_at = pl.ds(pl.multiple_of((1 - c) * 192, 64), 192)
    six = pl.ds(0, IL)

    loads = [
        pltpu.make_async_copy(src, dst, in_sem.at[n])
        for n, (src, dst) in enumerate(
            (
                (pair_hbm, pair), (mask_hbm, mask_s), (mask6_hbm, mask_v), (in_gain_hbm, in_gain),
                (w_in_hbm, w_in), (out_gain_hbm, out_gain), (w_out_hbm, w_out),
            )
        )
    ]
    for load in loads:
        load.start()

    lr0[1] = jnp.zeros(lr0.shape[1:], BF16)

    bits = [r // 2**k % 2 for k in range(4)]

    def chunk_of(step):
        zh = r // 16
        flip = ORDER[-1]
        for n in range(CHUNKS - 1):
            flip = flip + jnp.where(step == n, ORDER[n] - ORDER[-1], 0)
        return 2 * ((zh // 2 + flip // 2) % 2) + (zh % 2 + flip % 2) % 2

    place = {"xhi": 1, "y0": 2, "y1": 4, "xlo": 8, "z0": 16}
    here = dict(zip(place, [xhi] + bits))
    free = [name for name in FREE if name not in FIXED]
    offsets = []
    for low in range(2 ** len(free) - 1, -1, -1):
        to = {name: 1 - here[name] if low >> k & 1 else here[name] for k, name in enumerate(free)}
        e = sum(to[name] * (place[name] // 2) for name in free if name != "xhi")
        offsets.append((low, e, to["xhi"]))

    def chips(g, group, step, visit):
        mine = step == CHUNKS - 1
        for name, value in zip(FIXED, group):
            mine = mine & (here[name] == value)
        base = g * 16 + sum(value * (place[name] // 2) for name, value in zip(FIXED, group))
        for low, e, h in offsets:
            visit(base + e, h, low == 0 and mine)

    barrier = pltpu.get_barrier_semaphore()
    pl.semaphore_signal(barrier, inc=1, device_id=partner, device_id_type=MESH)

    @pl.loop(0, CHUNKS)
    def _(step):
        def greet(e, h, mine):
            def signal():
                pl.semaphore_signal(barrier, inc=1, device_id=(e, h * 2 + c), device_id_type=MESH)

            if mine is False:
                signal()
            else:
                pl.when(jnp.logical_not(mine))(signal)

        for group in GROUPS:
            chips(chunk_of(step), group, step, greet)

    for load in loads:
        load.wait()

    def turn(u):
        for v in range(4):
            turned = w_in[u, v].astype(F32).T.astype(BF16)
            for g in range(CHUNKS):
                wt[u, g, v * CW : (v + 1) * CW, :] = turned[g * CW : (g + 1) * CW]
        gcol[u] = jnp.broadcast_to(out_gain[u : u + 1, :], (CH, CH)).T

    def norm(u, lo=0, n=3):
        at = pl.ds(lo * 128, n * 128)

        @pl.loop(0, IL, unroll=6)
        def _(i):
            val = zbuf[i, at]
            shifted = val.astype(F32) - dot(val, ones[...], NN) * (1.0 / CH)
            spread = dot((shifted * shifted).astype(BF16), ones[...], NN) * (1.0 / CH)
            xn[i, at] = (shifted * lax.rsqrt(spread + 1e-05) * in_gain[u : u + 1, :]).astype(BF16)

    def gates(u):
        @pl.loop(0, IL, unroll=6)
        def _(i):
            gate[i] = sigmoid(dot(xn[i], w_in[u, 4], NN))

    def to_own(src):
        @pl.loop(0, IL)
        def _(i):
            zbuf[i, 0:128] = src[i, main_at]
            zbuf[i, 128:256] = src[IL + i, main_at]
            zbuf[i, 256:320] = src[i, tail_at]
            zbuf[i, 320:384] = src[IL + i, tail_at]

    def project(u, g, lo, n):
        at = pl.ds(lo * 128, n * 128)

        @pl.loop(0, IL, unroll=6)
        def _(i):
            o = dot(wt[u, g], xn[i, at], NT)
            mask = pm[u, pl.ds(i, 1), at]
            for s in range(2):
                side = sigmoid(o[2 * s * CW : (2 * s + 1) * CW])
                side = side * o[(2 * s + 1) * CW : (2 * s + 2) * CW] * mask
                for k in range(n):
                    bf[s, k, pl.ds(i, CW, stride=8), :] = side[:, k * 128 : (k + 1) * 128]

        for s in range(2):
            for k in range(n):
                b[pl.ds(g * CW, CW), s, lo + k] = bf[s, k].reshape(CW, 8, 128).astype(BF16)

    def send(src, dst, send_sem, recv_sem, to, mine):
        def remote():
            pltpu.make_async_remote_copy(
                src, dst, send_sem, recv_sem, device_id=to, device_id_type=MESH
            ).start()

        if mine is False:
            remote()
        else:
            pl.when(jnp.logical_not(mine))(remote)

            @pl.when(mine)
            def _():
                pltpu.make_async_copy(src, dst, recv_sem).start()

    lane = lax.broadcasted_iota(jnp.int32, (1, 128), 1)
    row_mask = [mask_s[r * 12 + i].astype(F32) for i in range(2 * IL)]
    main = mask_v[pl.ds(xhi * 3 + 2 * c, 1), :].astype(F32)
    tile = mask_v[pl.ds(xhi * 3 + 1, 1), :].astype(F32)
    swapped = halves(tile[:, 64:], tile[:, :64])
    tail = jnp.where((lane < 64) == (c == 0), tile, swapped)
    for i in range(IL):
        pm[0, i : i + 1, 0:128] = main * row_mask[i]
        pm[0, i : i + 1, 128:256] = main * row_mask[IL + i]
        pm[0, i : i + 1, 256:384] = tail * jnp.where(lane < 64, row_mask[i], row_mask[IL + i])
        for k in range(3):
            cols = mask_v[pl.ds(xhi * 3 + k, 1), :].astype(F32)
            pm[1, i : i + 1, k * 128 : (k + 1) * 128] = cols * jnp.where(
                c == 0, row_mask[i], row_mask[IL + i]
            )

    ones[...] = jnp.ones_like(ones)
    turn(0)
    to_own(pair)
    norm(0)
    project(0, chunk_of(0), 0, 3)

    pl.semaphore_wait(barrier, 128)

    def project_send(u, lo, n, stage, parts):
        for turn, (side, sides) in enumerate(((0, 1), (1, 1)) if stage == 2 else ((0, 2),)):
            sides = pl.ds(side, sides)

            for k in range(len(GROUPS)):
                def post(e, h, mine):
                    if u == 0:
                        slot = lr0.at[sides, pl.ds(lo, n), xhi, r, six, :]
                    else:
                        slot = lr1.at[sides, pl.ds(xhi * 3 + lo, n), r, six, :]
                    send(
                        b.at[e * 2 + h, sides, pl.ds(lo, n), six, :], slot,
                        lr_send.at[u], lr_recv.at[u, stage + turn], (e, h * 2 + c), mine,
                    )

                @pl.loop(0, CHUNKS)
                def _(step):
                    g = chunk_of(step)
                    if k == 0 and turn == 0 and u == 0:
                        pl.when(step > 0)(lambda: project(u, g, *parts))
                    elif k == 0 and turn == 0 and parts:
                        project(u, g, *parts)
                    chips(g, GROUPS[k], step, post)

    def finish(u, lo, n):
        for k in range(lo, lo + n):
            tf[...] = tri[u, k].astype(F32).reshape(CH * 8, 128)
            at = pl.ds(k * 128, 128)
            for i in range(IL):
                val = tf[pl.ds(i, CH, stride=8), :]
                shifted = val - jnp.mean(val, axis=0, keepdims=True)
                spread = jnp.mean(shifted * shifted, axis=0, keepdims=True)
                normed = (shifted * lax.rsqrt(spread + 1e-05) * gcol[u]).astype(BF16)
                term = dot(normed, w_out[u], TN) * gate[i, at, :]
                zbuf[i, at, :] = (zbuf[i, at, :].astype(F32) + term).astype(BF16)

    def lr_sent(u):
        most = b.at[pl.ds(0, CH - 1), :, :, six, :]
        pltpu.make_async_copy(most, most, lr_send.at[u]).wait()

    def t_sent(u):
        most = tri.at[u, :, pl.ds(0, CH - 1), six, :]
        pltpu.make_async_copy(most, most, t_send.at[u]).wait()

    for u in range(2):
        if u == 0:
            project_send(0, 0, 3, 0, (0, 3))

        if u == 0:
            swap = pltpu.make_async_remote_copy(
                pair.at[pl.ds((1 - c) * IL, IL)], zin.at[...], x_send.at[0], x_recv.at[0],
                device_id=partner, device_id_type=MESH,
            )
            swap.start()
            lr1[...] = jnp.zeros_like(lr1)
            turn(1)
            k_id = lax.broadcasted_iota(jnp.int32, (512, 384), 0)
            i_id = lax.broadcasted_iota(jnp.int32, (512, 384), 1)
            row = k_id % 256 // 8 * 12 + k_id // 256 * IL + k_id % 8
            sel[...] = jnp.where((k_id % 8 < IL) & (row == i_id), 1.0, 0.0).astype(BF16)
            k_id = lax.broadcasted_iota(jnp.int32, (384, 512), 1)
            i_id = lax.broadcasted_iota(jnp.int32, (384, 512), 0)
            row = k_id % 256 // 8 * 12 + k_id // 256 * IL + k_id % 8
            selt[...] = jnp.where((k_id % 8 < IL) & (row == i_id), 1.0, 0.0).astype(BF16)
            swap.wait()
            zbuf[:, mine_at, :] = pair[pl.ds(c * IL, IL)]
            zbuf[:, other_at, :] = zin[...]
        else:
            swap = pltpu.make_async_remote_copy(
                zbuf.at[:, other_at, :], zown.at[pl.ds(c * IL, IL)], x_send.at[1], x_recv.at[1],
                device_id=partner, device_id_type=MESH,
            )
            swap.start()
            zown[pl.ds(c * IL, IL)] = zbuf[:, mine_at, :]
            swap.wait()
            to_own(zown)
        norm(u)
        gates(u)

        def received(stage, ref):
            pltpu.make_async_copy(ref, ref, lr_recv.at[u, stage]).wait()

        if u == 0:
            received(0, b.at[:, :, :, six, :])
        else:
            for stage in range(3):
                received(stage, b.at[:, 0 : 1 if stage == 2 else 2, 0, six, :])


        if u == 0:
            xs, xp = xs0, xp0
            for s in range(2):
                t0, t1 = lr0[s, 2, 0].reshape(512, 128), lr0[s, 2, 1].reshape(512, 128)
                tl[s, 0] = halves(t0[:, :64], t1[:, :64])
                tl[s, 1] = halves(t0[:, 64:], t1[:, 64:])
            for half in range(2):
                at = slice(half * 32, half * 32 + 32)
                parts = [
                    jnp.concatenate(
                        [lr0[1, d, 0, at].reshape(256, 128), lr0[1, d, 1, at].reshape(256, 128),
                         tl[1, d, half * 256 : half * 256 + 256]], axis=1,
                    )
                    for d in range(2)
                ]
                rc[384 * half : 384 * half + 384, :] = dot(
                    selt[...], jnp.concatenate(parts, axis=0), NN
                ).astype(BF16)

            def product(d, n):
                at = pl.ds(n * 16, 16)
                left = [lr0[0, d, h, at].reshape(128, 128) for h in range(2)]
                left.append(tl[0, d, pl.ds(pl.multiple_of(n * 128, 128), 128), :])
                return dot(jnp.concatenate(left, axis=1), rc[...], NT)
        else:
            xs, xp = xs1, xp1
            for half in range(2):
                part = [lr1[0, half * 3 + k].reshape(512, 128) for k in range(3)]
                turned = dot(sel[...], jnp.concatenate(part, axis=1), NT).astype(BF16)
                for d in range(2):
                    lt[d, half * 256 : half * 256 + 256] = turned[d * 256 : d * 256 + 256]
            def product(d, n):
                at = pl.ds(pl.multiple_of(n * 128, 128), 128)
                left = jnp.concatenate([lt[0, at], lt[1, at]], axis=0)
                right = [lr1[1, h * 3 + 2 * d].reshape(512, 128) for h in range(2)]
                return dot(left, jnp.concatenate(right, axis=1), NN)

            def product_tail(d, n):
                at = pl.ds(pl.multiple_of(n * 128, 128), 128)
                left = jnp.concatenate([lt[0, at], lt[1, at]], axis=0)
                return dot(left, tl[0, d], NN)

        def give(n, tail=False):
            here, there = (xst, xpt) if tail else (xs, xp)
            row = 2 if tail else u
            return pltpu.make_async_remote_copy(
                here.at[n], there.at[n], p_send.at[row, n], p_recv.at[row, n],
                device_id=partner, device_id_type=MESH,
            )

        @pl.loop(0, CHUNKS, unroll=4)
        def _(step):
            n = chunk_of(step)
            xs[n] = product(1 - c, n).astype(BF16)
            give(n).start()

        def back(stage):
            lo, n = STAGES[u][stage]

            def post(e, h, mine):
                send(
                    ts.at[e, h, pl.ds(lo, n), six, :], tri.at[u, pl.ds(lo, n), chip, six, :],
                    t_send.at[u], t_recv.at[u, stage], (e, h * 2 + c), mine,
                )

            return post

        if u == 1:
            t_sent(0)

        @pl.loop(0, CHUNKS)
        def _(step):
            n = chunk_of(step)
            p = product(c, n)
            give(n).wait_recv()
            p = p + xp[n].astype(F32)
            at = pl.ds(n * 16, 16)
            if u == 0:
                for h in range(2):
                    for k in range(3):
                        tile = p[:, (h * 3 + k) * 128 : (h * 3 + k + 1) * 128]
                        ts[at, h, k] = tile.reshape(16, 8, 128).astype(BF16)
            else:
                low, high = p[0:128], p[128:256]
                for h in range(2):
                    ts[at, h, 0] = low[:, h * 128 : h * 128 + 128].reshape(16, 8, 128).astype(BF16)
                    ts[at, h, 1] = high[:, h * 128 : h * 128 + 128].reshape(16, 8, 128).astype(BF16)

            for group in GROUPS[:4]:
                chips(n, group, step, back(0))

        for k in range(4, len(GROUPS)):
            @pl.loop(0, CHUNKS)
            def _(step):
                chips(chunk_of(step), GROUPS[k], step, back(0))

        if u == 1:
            received(3, b.at[:, 0:1, 0, six, :])
            t0, t1 = lr1[1, 1].reshape(512, 128), lr1[1, 4].reshape(512, 128)
            tl[0, 0] = halves(t0[:, :64], t1[:, :64])
            tl[0, 1] = halves(t0[:, 64:], t1[:, 64:])

            @pl.loop(0, CHUNKS, unroll=4)
            def _(step):
                n = chunk_of(step)
                xst[n] = product_tail(1 - c, n).astype(BF16)
                give(n, True).start()

            @pl.loop(0, CHUNKS)
            def _(step):
                n = chunk_of(step)
                p = product_tail(c, n)
                give(n, True).wait_recv()
                p = p + xpt[n].astype(F32)
                low, high = p[0:128], p[128:256]
                for h in range(2):
                    cols = slice(h * 64, h * 64 + 64)
                    tile = halves(low[:, cols], high[:, cols])
                    ts[pl.ds(n * 16, 16), h, 2] = tile.reshape(16, 8, 128).astype(BF16)

        for stage in range(1, len(STAGES[u])):
            for k in range(len(GROUPS)):
                @pl.loop(0, CHUNKS)
                def _(step):
                    chips(chunk_of(step), GROUPS[k], step, back(stage))

        for n in range(CHUNKS):
            give(n).wait_send()
            if u == 1:
                give(n, True).wait_send()
        for stage, (lo, n) in enumerate(STAGES[u]):
            part = tri.at[u, pl.ds(lo, n), :, six, :]
            pltpu.make_async_copy(part, part, t_recv.at[u, stage]).wait()
            finish(u, lo, n)
            if u == 0:
                norm(1, lo, n)
                if stage == 0:
                    lr_sent(0)
                if stage == 0:
                    project_send(1, 0, 1, 0, (0, 1))
                else:
                    project_send(1, 2, 1, 1, (1, 2))
                    project_send(1, 1, 1, 2, None)
    lr_sent(1)
    t_sent(1)

    @pl.loop(0, IL)
    def _(i):
        out_ref[i, main_at] = zbuf[i, 0:128]
        out_ref[IL + i, main_at] = zbuf[i, 128:256]
        out_ref[i, tail_at] = zbuf[i, 256:320]
        out_ref[IL + i, tail_at] = zbuf[i, 320:384]


def on_device(pair, residue_mask, in_gain, w_in, out_gain, w_out):
    hbm = pl.BlockSpec(memory_space=pl.ANY)
    dma = pltpu.SemaphoreType.DMA
    return pl.pallas_call(
        kernel,
        out_shape=jax.ShapeDtypeStruct(pair.shape, BF16),
        in_specs=[hbm] * 7,
        out_specs=pl.BlockSpec(memory_space=pltpu.VMEM),
        scratch_shapes=[
            pltpu.VMEM(pair.shape, BF16),
            pltpu.SMEM((768,), jnp.int32),
            pltpu.VMEM((6, 128), jnp.int32),
            pltpu.VMEM(in_gain.shape, F32),
            pltpu.VMEM(w_in.shape, BF16),
            pltpu.VMEM(out_gain.shape, F32),
            pltpu.VMEM(w_out.shape, BF16),
            pltpu.VMEM((IL, 192, CH), BF16),
            pltpu.VMEM((IL, 384, CH), BF16),
            pltpu.VMEM((2 * IL, 192, CH), BF16),
            pltpu.VMEM((IL, 384, CH), BF16),
            pltpu.VMEM((IL, 384, CH), F32),
            pltpu.VMEM((2, CHUNKS, 4 * CW, CH), BF16),
            pltpu.VMEM((2, 3, CW * 8, 128), F32),
            pltpu.VMEM((CH, 2, 3, 8, 128), BF16),
            pltpu.VMEM((2, 3, 2, 64, 8, 128), BF16),
            pltpu.VMEM((2, 6, 64, 8, 128), BF16),
            pltpu.VMEM((768, 384), BF16),
            pltpu.VMEM((2, 512, 512), BF16),
            pltpu.VMEM((2, 2, 512, 128), BF16),
            pltpu.VMEM((512, 384), BF16),
            pltpu.VMEM((384, 512), BF16),
            pltpu.VMEM((4, 128, 768), BF16),
            pltpu.VMEM((4, 128, 768), BF16),
            pltpu.VMEM((4, 256, 256), BF16),
            pltpu.VMEM((4, 256, 256), BF16),
            pltpu.VMEM((4, 256, 128), BF16),
            pltpu.VMEM((4, 256, 128), BF16),
            pltpu.VMEM((64, 2, 3, 8, 128), BF16),
            pltpu.VMEM((2, 3, CH, 8, 128), BF16),
            pltpu.VMEM((CH * 8, 128), F32),
            pltpu.VMEM((2, CH, 128), F32),
            pltpu.VMEM((2, 8, 384), F32),
            pltpu.VMEM((CH, 128), BF16),
            dma((7,)), dma((2,)), dma((2,)), dma((3, 4)), dma((3, 4)),
            dma((2,)), dma((2, 4)), dma((2,)), dma((2, 3)),
        ],
        compiler_params=pltpu.CompilerParams(
            collective_id=0, has_side_effects=True, vmem_limit_bytes=62 * 2**20
        ),
        name="triangle",
    )(pair, residue_mask, residue_mask.reshape(6, 128), in_gain, w_in, out_gain, w_out)


def solution(mesh):
    placed = (P("row", "col", None), P(), P(), P(), P(), P())
    return jax.shard_map(
        on_device, mesh=mesh, in_specs=placed, out_specs=P("row", "col", None), check_vma=False
    )
```

```python
import jax
import jax.numpy as jnp
from jax import lax
from jax.experimental import pallas as pl
from jax.experimental.pallas import tpu as pltpu
from jax.sharding import PartitionSpec as P

MESH = pl.DeviceIdType.MESH
F32 = jnp.float32
BF16 = jnp.bfloat16
CH = 128
IL = 6
CHUNKS = 4
CW = CH // CHUNKS
ORDER = (2, 3, 1, 0)
FIXED = ("z0", "y0")
GROUPS = ((0, 0), (1, 1), (0, 1), (1, 0))
FREE = ("xhi", "y0", "y1", "xlo", "z0")
STAGES = (((0, 1), (1, 2)), ((0, 2), (2, 1)))
NT = (((1,), (1,)), ((), ()))
NN = (((1,), (0,)), ((), ()))
TN = (((0,), (0,)), ((), ()))


def dot(a, b, dims):
    return lax.dot_general(a, b, dims, preferred_element_type=F32)


def sigmoid(v):
    return 0.5 * jnp.tanh(0.5 * v) + 0.5


def halves(a, b):
    return jnp.concatenate([a, b], axis=1)


def kernel(
    pair_hbm, mask_hbm, mask6_hbm, in_gain_hbm, w_in_hbm, out_gain_hbm, w_out_hbm, out_ref,
    pair, mask_s, mask_v, in_gain, w_in, out_gain, w_out,
    zin, zbuf, zown, xn, gate, wt, bf, b, lr0, lr1, rc, lt, tl, sel, selt, xs0, xp0, xs1, xp1, xst, xpt,
    ts, tri, tf, gcol, pm, ones,
    in_sem, x_send, x_recv, p_send, p_recv, lr_send, lr_recv, t_send, t_recv,
):
    r = lax.axis_index("row")
    q = lax.axis_index("col")
    xhi = q // 2
    c = q % 2
    partner = (r, xhi * 2 + 1 - c)
    chip = r * 2 + xhi
    main_at = pl.ds(pl.multiple_of(c * 64, 64), 128)
    tail_at = pl.ds(pl.multiple_of((1 - c) * 128, 128), 64)
    mine_at = pl.ds(pl.multiple_of(c * 192, 64), 192)
    other_at = pl.ds(pl.multiple_of((1 - c) * 192, 64), 192)
    six = pl.ds(0, IL)

    loads = [
        pltpu.make_async_copy(src, dst, in_sem.at[n])
        for n, (src, dst) in enumerate(
            (
                (pair_hbm, pair), (mask_hbm, mask_s), (mask6_hbm, mask_v), (in_gain_hbm, in_gain),
                (w_in_hbm, w_in), (out_gain_hbm, out_gain), (w_out_hbm, w_out),
            )
        )
    ]
    for load in loads:
        load.start()

    lr0[1] = jnp.zeros(lr0.shape[1:], BF16)

    bits = [r // 2**k % 2 for k in range(4)]

    def chunk_of(step):
        zh = r // 16
        flip = ORDER[-1]
        for n in range(CHUNKS - 1):
            flip = flip + jnp.where(step == n, ORDER[n] - ORDER[-1], 0)
        return 2 * ((zh // 2 + flip // 2) % 2) + (zh % 2 + flip % 2) % 2

    place = {"xhi": 1, "y0": 2, "y1": 4, "xlo": 8, "z0": 16}
    here = dict(zip(place, [xhi] + bits))
    free = [name for name in FREE if name not in FIXED]
    offsets = []
    for low in range(2 ** len(free) - 1, -1, -1):
        to = {name: 1 - here[name] if low >> k & 1 else here[name] for k, name in enumerate(free)}
        e = sum(to[name] * (place[name] // 2) for name in free if name != "xhi")
        offsets.append((low, e, to["xhi"]))

    def chips(g, group, step, visit):
        mine = step == CHUNKS - 1
        for name, value in zip(FIXED, group):
            mine = mine & (here[name] == value)
        base = g * 16 + sum(value * (place[name] // 2) for name, value in zip(FIXED, group))
        for low, e, h in offsets:
            visit(base + e, h, low == 0 and mine)

    barrier = pltpu.get_barrier_semaphore()
    pl.semaphore_signal(barrier, inc=1, device_id=partner, device_id_type=MESH)

    @pl.loop(0, CHUNKS)
    def _(step):
        def greet(e, h, mine):
            def signal():
                pl.semaphore_signal(barrier, inc=1, device_id=(e, h * 2 + c), device_id_type=MESH)

            if mine is False:
                signal()
            else:
                pl.when(jnp.logical_not(mine))(signal)

        for group in GROUPS:
            chips(chunk_of(step), group, step, greet)

    for load in loads:
        load.wait()

    def turn(u):
        for v in range(4):
            turned = w_in[u, v].astype(F32).T.astype(BF16)
            for g in range(CHUNKS):
                wt[u, g, v * CW : (v + 1) * CW, :] = turned[g * CW : (g + 1) * CW]
        gcol[u] = jnp.broadcast_to(out_gain[u : u + 1, :], (CH, CH)).T

    def norm(u, lo=0, n=3):
        at = pl.ds(lo * 128, n * 128)

        @pl.loop(0, IL, unroll=6)
        def _(i):
            val = zbuf[i, at]
            shifted = val.astype(F32) - dot(val, ones[...], NN) * (1.0 / CH)
            spread = dot((shifted * shifted).astype(BF16), ones[...], NN) * (1.0 / CH)
            xn[i, at] = (shifted * lax.rsqrt(spread + 1e-05) * in_gain[u : u + 1, :]).astype(BF16)

    def gates(u):
        @pl.loop(0, IL, unroll=6)
        def _(i):
            gate[i] = sigmoid(dot(xn[i], w_in[u, 4], NN))

    def to_own(src):
        @pl.loop(0, IL)
        def _(i):
            zbuf[i, 0:128] = src[i, main_at]
            zbuf[i, 128:256] = src[IL + i, main_at]
            zbuf[i, 256:320] = src[i, tail_at]
            zbuf[i, 320:384] = src[IL + i, tail_at]

    def project(u, g, lo, n):
        at = pl.ds(lo * 128, n * 128)

        @pl.loop(0, IL, unroll=6)
        def _(i):
            o = dot(wt[u, g], xn[i, at], NT)
            mask = pm[u, pl.ds(i, 1), at]
            for s in range(2):
                side = sigmoid(o[2 * s * CW : (2 * s + 1) * CW])
                side = side * o[(2 * s + 1) * CW : (2 * s + 2) * CW] * mask
                for k in range(n):
                    bf[s, k, pl.ds(i, CW, stride=8), :] = side[:, k * 128 : (k + 1) * 128]

        for s in range(2):
            for k in range(n):
                b[pl.ds(g * CW, CW), s, lo + k] = bf[s, k].reshape(CW, 8, 128).astype(BF16)

    def send(src, dst, send_sem, recv_sem, to, mine):
        def remote():
            pltpu.make_async_remote_copy(
                src, dst, send_sem, recv_sem, device_id=to, device_id_type=MESH
            ).start()

        if mine is False:
            remote()
        else:
            pl.when(jnp.logical_not(mine))(remote)

            @pl.when(mine)
            def _():
                pltpu.make_async_copy(src, dst, recv_sem).start()

    lane = lax.broadcasted_iota(jnp.int32, (1, 128), 1)
    row_mask = [mask_s[r * 12 + i].astype(F32) for i in range(2 * IL)]
    main = mask_v[pl.ds(xhi * 3 + 2 * c, 1), :].astype(F32)
    tile = mask_v[pl.ds(xhi * 3 + 1, 1), :].astype(F32)
    swapped = halves(tile[:, 64:], tile[:, :64])
    tail = jnp.where((lane < 64) == (c == 0), tile, swapped)
    for i in range(IL):
        pm[0, i : i + 1, 0:128] = main * row_mask[i]
        pm[0, i : i + 1, 128:256] = main * row_mask[IL + i]
        pm[0, i : i + 1, 256:384] = tail * jnp.where(lane < 64, row_mask[i], row_mask[IL + i])
        for k in range(3):
            cols = mask_v[pl.ds(xhi * 3 + k, 1), :].astype(F32)
            pm[1, i : i + 1, k * 128 : (k + 1) * 128] = cols * jnp.where(
                c == 0, row_mask[i], row_mask[IL + i]
            )

    ones[...] = jnp.ones_like(ones)
    turn(0)
    to_own(pair)
    norm(0)
    @pl.loop(0, CHUNKS)
    def _(step):
        project(0, chunk_of(step), 0, 3)

    pl.semaphore_wait(barrier, 128)

    def project_send(u, lo, n, stage, parts):
        for turn, (side, sides) in enumerate(((0, 1), (1, 1)) if stage == 2 else ((0, 2),)):
            sides = pl.ds(side, sides)

            for k in range(len(GROUPS)):
                def post(e, h, mine):
                    if u == 0:
                        slot = lr0.at[sides, pl.ds(lo, n), xhi, r, six, :]
                    else:
                        slot = lr1.at[sides, pl.ds(xhi * 3 + lo, n), r, six, :]
                    send(
                        b.at[e * 2 + h, sides, pl.ds(lo, n), six, :], slot,
                        lr_send.at[u], lr_recv.at[u, stage + turn], (e, h * 2 + c), mine,
                    )

                @pl.loop(0, CHUNKS)
                def _(step):
                    g = chunk_of(step)
                    if k == 0 and turn == 0 and u == 1 and parts:
                        project(u, g, *parts)
                    chips(g, GROUPS[k], step, post)

    def finish(u, lo, n):
        for k in range(lo, lo + n):
            tf[...] = tri[u, k].astype(F32).reshape(CH * 8, 128)
            at = pl.ds(k * 128, 128)
            for i in range(IL):
                val = tf[pl.ds(i, CH, stride=8), :]
                shifted = val - jnp.mean(val, axis=0, keepdims=True)
                spread = jnp.mean(shifted * shifted, axis=0, keepdims=True)
                normed = (shifted * lax.rsqrt(spread + 1e-05) * gcol[u]).astype(BF16)
                term = dot(normed, w_out[u], TN) * gate[i, at, :]
                zbuf[i, at, :] = (zbuf[i, at, :].astype(F32) + term).astype(BF16)

    def lr_sent(u):
        most = b.at[pl.ds(0, CH - 1), :, :, six, :]
        pltpu.make_async_copy(most, most, lr_send.at[u]).wait()

    def t_sent(u):
        most = tri.at[u, :, pl.ds(0, CH - 1), six, :]
        pltpu.make_async_copy(most, most, t_send.at[u]).wait()

    for u in range(2):
        if u == 0:
            project_send(0, 0, 3, 0, (0, 3))

        if u == 0:
            swap = pltpu.make_async_remote_copy(
                pair.at[pl.ds((1 - c) * IL, IL)], zin.at[...], x_send.at[0], x_recv.at[0],
                device_id=partner, device_id_type=MESH,
            )
            swap.start()
            lr1[...] = jnp.zeros_like(lr1)
            turn(1)
            k_id = lax.broadcasted_iota(jnp.int32, (512, 384), 0)
            i_id = lax.broadcasted_iota(jnp.int32, (512, 384), 1)
            row = k_id % 256 // 8 * 12 + k_id // 256 * IL + k_id % 8
            sel[...] = jnp.where((k_id % 8 < IL) & (row == i_id), 1.0, 0.0).astype(BF16)
            k_id = lax.broadcasted_iota(jnp.int32, (384, 512), 1)
            i_id = lax.broadcasted_iota(jnp.int32, (384, 512), 0)
            row = k_id % 256 // 8 * 12 + k_id // 256 * IL + k_id % 8
            selt[...] = jnp.where((k_id % 8 < IL) & (row == i_id), 1.0, 0.0).astype(BF16)
            swap.wait()
            zbuf[:, mine_at, :] = pair[pl.ds(c * IL, IL)]
            zbuf[:, other_at, :] = zin[...]
        else:
            swap = pltpu.make_async_remote_copy(
                zbuf.at[:, other_at, :], zown.at[pl.ds(c * IL, IL)], x_send.at[1], x_recv.at[1],
                device_id=partner, device_id_type=MESH,
            )
            swap.start()
            zown[pl.ds(c * IL, IL)] = zbuf[:, mine_at, :]
            swap.wait()
            to_own(zown)
        norm(u)
        gates(u)

        def received(stage, ref):
            pltpu.make_async_copy(ref, ref, lr_recv.at[u, stage]).wait()

        if u == 0:
            received(0, b.at[:, :, :, six, :])
        else:
            for stage in range(3):
                received(stage, b.at[:, 0 : 1 if stage == 2 else 2, 0, six, :])


        if u == 0:
            xs, xp = xs0, xp0
            for s in range(2):
                t0, t1 = lr0[s, 2, 0].reshape(512, 128), lr0[s, 2, 1].reshape(512, 128)
                tl[s, 0] = halves(t0[:, :64], t1[:, :64])
                tl[s, 1] = halves(t0[:, 64:], t1[:, 64:])
            for half in range(2):
                at = slice(half * 32, half * 32 + 32)
                parts = [
                    jnp.concatenate(
                        [lr0[1, d, 0, at].reshape(256, 128), lr0[1, d, 1, at].reshape(256, 128),
                         tl[1, d, half * 256 : half * 256 + 256]], axis=1,
                    )
                    for d in range(2)
                ]
                rc[384 * half : 384 * half + 384, :] = dot(
                    selt[...], jnp.concatenate(parts, axis=0), NN
                ).astype(BF16)

            def product(d, n):
                at = pl.ds(n * 16, 16)
                left = [lr0[0, d, h, at].reshape(128, 128) for h in range(2)]
                left.append(tl[0, d, pl.ds(pl.multiple_of(n * 128, 128), 128), :])
                return dot(jnp.concatenate(left, axis=1), rc[...], NT)
        else:
            xs, xp = xs1, xp1
            for half in range(2):
                part = [lr1[0, half * 3 + k].reshape(512, 128) for k in range(3)]
                turned = dot(sel[...], jnp.concatenate(part, axis=1), NT).astype(BF16)
                for d in range(2):
                    lt[d, half * 256 : half * 256 + 256] = turned[d * 256 : d * 256 + 256]
            def product(d, n):
                at = pl.ds(pl.multiple_of(n * 128, 128), 128)
                left = jnp.concatenate([lt[0, at], lt[1, at]], axis=0)
                right = [lr1[1, h * 3 + 2 * d].reshape(512, 128) for h in range(2)]
                return dot(left, jnp.concatenate(right, axis=1), NN)

            def product_tail(d, n):
                at = pl.ds(pl.multiple_of(n * 128, 128), 128)
                left = jnp.concatenate([lt[0, at], lt[1, at]], axis=0)
                return dot(left, tl[0, d], NN)

        def give(n, tail=False):
            here, there = (xst, xpt) if tail else (xs, xp)
            row = 2 if tail else u
            return pltpu.make_async_remote_copy(
                here.at[n], there.at[n], p_send.at[row, n], p_recv.at[row, n],
                device_id=partner, device_id_type=MESH,
            )

        @pl.loop(0, CHUNKS, unroll=4)
        def _(step):
            n = chunk_of(step)
            xs[n] = product(1 - c, n).astype(BF16)
            give(n).start()

        def back(stage):
            lo, n = STAGES[u][stage]

            def post(e, h, mine):
                send(
                    ts.at[e, h, pl.ds(lo, n), six, :], tri.at[u, pl.ds(lo, n), chip, six, :],
                    t_send.at[u], t_recv.at[u, stage], (e, h * 2 + c), mine,
                )

            return post

        if u == 1:
            t_sent(0)

        @pl.loop(0, CHUNKS)
        def _(step):
            n = chunk_of(step)
            p = product(c, n)
            give(n).wait_recv()
            p = p + xp[n].astype(F32)
            at = pl.ds(n * 16, 16)
            if u == 0:
                for h in range(2):
                    for k in range(3):
                        tile = p[:, (h * 3 + k) * 128 : (h * 3 + k + 1) * 128]
                        ts[at, h, k] = tile.reshape(16, 8, 128).astype(BF16)
            else:
                low, high = p[0:128], p[128:256]
                for h in range(2):
                    ts[at, h, 0] = low[:, h * 128 : h * 128 + 128].reshape(16, 8, 128).astype(BF16)
                    ts[at, h, 1] = high[:, h * 128 : h * 128 + 128].reshape(16, 8, 128).astype(BF16)

            for group in GROUPS[:4]:
                chips(n, group, step, back(0))

        for k in range(4, len(GROUPS)):
            @pl.loop(0, CHUNKS)
            def _(step):
                chips(chunk_of(step), GROUPS[k], step, back(0))

        if u == 1:
            received(3, b.at[:, 0:1, 0, six, :])
            t0, t1 = lr1[1, 1].reshape(512, 128), lr1[1, 4].reshape(512, 128)
            tl[0, 0] = halves(t0[:, :64], t1[:, :64])
            tl[0, 1] = halves(t0[:, 64:], t1[:, 64:])

            @pl.loop(0, CHUNKS, unroll=4)
            def _(step):
                n = chunk_of(step)
                xst[n] = product_tail(1 - c, n).astype(BF16)
                give(n, True).start()

            @pl.loop(0, CHUNKS)
            def _(step):
                n = chunk_of(step)
                p = product_tail(c, n)
                give(n, True).wait_recv()
                p = p + xpt[n].astype(F32)
                low, high = p[0:128], p[128:256]
                for h in range(2):
                    cols = slice(h * 64, h * 64 + 64)
                    tile = halves(low[:, cols], high[:, cols])
                    ts[pl.ds(n * 16, 16), h, 2] = tile.reshape(16, 8, 128).astype(BF16)

        for stage in range(1, len(STAGES[u])):
            for k in range(len(GROUPS)):
                @pl.loop(0, CHUNKS)
                def _(step):
                    chips(chunk_of(step), GROUPS[k], step, back(stage))

        for n in range(CHUNKS):
            give(n).wait_send()
            if u == 1:
                give(n, True).wait_send()
        for stage, (lo, n) in enumerate(STAGES[u]):
            part = tri.at[u, pl.ds(lo, n), :, six, :]
            pltpu.make_async_copy(part, part, t_recv.at[u, stage]).wait()
            finish(u, lo, n)
            if u == 0:
                norm(1, lo, n)
                if stage == 0:
                    lr_sent(0)
                if stage == 0:
                    project_send(1, 0, 1, 0, (0, 1))
                else:
                    project_send(1, 2, 1, 1, (1, 2))
                    project_send(1, 1, 1, 2, None)
    lr_sent(1)
    t_sent(1)

    @pl.loop(0, IL)
    def _(i):
        out_ref[i, main_at] = zbuf[i, 0:128]
        out_ref[IL + i, main_at] = zbuf[i, 128:256]
        out_ref[i, tail_at] = zbuf[i, 256:320]
        out_ref[IL + i, tail_at] = zbuf[i, 320:384]


def on_device(pair, residue_mask, in_gain, w_in, out_gain, w_out):
    hbm = pl.BlockSpec(memory_space=pl.ANY)
    dma = pltpu.SemaphoreType.DMA
    return pl.pallas_call(
        kernel,
        out_shape=jax.ShapeDtypeStruct(pair.shape, BF16),
        in_specs=[hbm] * 7,
        out_specs=pl.BlockSpec(memory_space=pltpu.VMEM),
        scratch_shapes=[
            pltpu.VMEM(pair.shape, BF16),
            pltpu.SMEM((768,), jnp.int32),
            pltpu.VMEM((6, 128), jnp.int32),
            pltpu.VMEM(in_gain.shape, F32),
            pltpu.VMEM(w_in.shape, BF16),
            pltpu.VMEM(out_gain.shape, F32),
            pltpu.VMEM(w_out.shape, BF16),
            pltpu.VMEM((IL, 192, CH), BF16),
            pltpu.VMEM((IL, 384, CH), BF16),
            pltpu.VMEM((2 * IL, 192, CH), BF16),
            pltpu.VMEM((IL, 384, CH), BF16),
            pltpu.VMEM((IL, 384, CH), F32),
            pltpu.VMEM((2, CHUNKS, 4 * CW, CH), BF16),
            pltpu.VMEM((2, 3, CW * 8, 128), F32),
            pltpu.VMEM((CH, 2, 3, 8, 128), BF16),
            pltpu.VMEM((2, 3, 2, 64, 8, 128), BF16),
            pltpu.VMEM((2, 6, 64, 8, 128), BF16),
            pltpu.VMEM((768, 384), BF16),
            pltpu.VMEM((2, 512, 512), BF16),
            pltpu.VMEM((2, 2, 512, 128), BF16),
            pltpu.VMEM((512, 384), BF16),
            pltpu.VMEM((384, 512), BF16),
            pltpu.VMEM((4, 128, 768), BF16),
            pltpu.VMEM((4, 128, 768), BF16),
            pltpu.VMEM((4, 256, 256), BF16),
            pltpu.VMEM((4, 256, 256), BF16),
            pltpu.VMEM((4, 256, 128), BF16),
            pltpu.VMEM((4, 256, 128), BF16),
            pltpu.VMEM((64, 2, 3, 8, 128), BF16),
            pltpu.VMEM((2, 3, CH, 8, 128), BF16),
            pltpu.VMEM((CH * 8, 128), F32),
            pltpu.VMEM((2, CH, 128), F32),
            pltpu.VMEM((2, 8, 384), F32),
            pltpu.VMEM((CH, 128), BF16),
            dma((7,)), dma((2,)), dma((2,)), dma((3, 4)), dma((3, 4)),
            dma((2,)), dma((2, 4)), dma((2,)), dma((2, 3)),
        ],
        compiler_params=pltpu.CompilerParams(
            collective_id=0, has_side_effects=True, vmem_limit_bytes=62 * 2**20
        ),
        name="triangle",
    )(pair, residue_mask, residue_mask.reshape(6, 128), in_gain, w_in, out_gain, w_out)


def solution(mesh):
    placed = (P("row", "col", None), P(), P(), P(), P(), P())
    return jax.shard_map(
        on_device, mesh=mesh, in_specs=placed, out_specs=P("row", "col", None), check_vma=False
    )
```
